128 devices in a mesh: sa: 8 (over z, y_hi), sb: 16 (over x, y_lo, core).
Axes of the slice: x: 4, y: 4 (y_hi: 2, y_lo: 2; y = y_hi * 2 + y_lo), z: 4, core: 2. Of those that a mesh axis runs over, the one named last changes fastest.
Arguments:
- queries: float32 [32768, 128], P(('sa', 'sb')), may hold values from -6 to 6
- keys: float32 [32768, 128], P(('sa', 'sb')), may hold values from -6 to 6
- values: float32 [32768, 128], P(('sa', 'sb')), may hold values from -6 to 6
- cotangent: float32 [32768, 128], P(('sa', 'sb')), may hold values from -6 to 6
- filt: float32 [32768, 128], P(('sa', 'sb')), may hold values from -6 to 6
- skip: float32 [128], replicated, may hold values from -4 to 4
Outputs:
- grad_queries: float32 [32768, 128], P(('sa', 'sb'))
- grad_keys: float32 [32768, 128], P(('sa', 'sb'))
- grad_values: float32 [32768, 128], P(('sa', 'sb'))
- grad_filter: float32 [32768, 128], P(('sa', 'sb'))
The draws below stay inside these ranges and needn't reach their ends.
All inputs are finite; a program needn't handle non-finite values.
Results may differ from the reference program's by a relative error of at most 0.000098.
Values sent between devices are 32-bit elements; how exact they have to be, the bound alone decides.
A program may use at most 64 MiB of HBM per device.

```python
import jax
import jax.numpy as jnp

CH = 128
TOKENS = 32768


def shard_levels(stream_key, dims, pieces, least, top_value):
    def one(axis_at, parts):
        draws = jax.random.uniform(jax.random.fold_in(jax.random.fold_in(stream_key, 6), axis_at), (parts,), jnp.float32, least / len(pieces), top_value / len(pieces))
        return jnp.repeat(jnp.exp(draws), dims[axis_at] // parts).reshape((-1,) + (1,) * (len(dims) - axis_at - 1))

    loudness = one(*pieces[0])
    for cut in pieces[1:]:
        loudness = loudness * one(*cut)
    return loudness


def noise(key, extent, spread, most, split=(), kind=jnp.bfloat16):
    values = jax.random.normal(key, extent, jnp.float32) * spread
    if len(split) > 0:
        values = shard_levels(key, extent, split, -0.22, 0.18) * values
    return jnp.clip(values, min=-most, max=most).astype(kind)


def setup_inputs(seed: int = 0) -> dict:
    arg_keys = jax.random.split(jax.random.key(seed), 7)
    return {
        "queries": noise(arg_keys[0], (TOKENS, CH), 1.0, 6.0, ((0, 128),), jnp.float32),
        "keys": noise(arg_keys[1], (TOKENS, CH), 1.0, 6.0, ((0, 128),), jnp.float32),
        "values": noise(arg_keys[2], (TOKENS, CH), 1.0, 6.0, ((0, 128),), jnp.float32),
        "cotangent": noise(arg_keys[3], (TOKENS, CH), 1.0, 6.0, ((0, 128),), jnp.float32),
        "filt": noise(arg_keys[4], (TOKENS, CH), 1.0, 6.0, ((0, 128),), jnp.float32),
        "skip": noise(arg_keys[5], (CH,), 1.0, 4.0, (), jnp.float32),
    }


def reference(queries, keys, values, cotangent, filt, skip):
    tokens = queries.shape[0]
    scaling = 1.0 / jnp.sqrt(jnp.float32(tokens))
    gated = keys * values
    upstream = cotangent * queries
    padded = 2 * tokens
    spectrum_gated = jnp.fft.fft(gated, n=padded, axis=0)
    spectrum_filter = jnp.fft.fft(filt, n=padded, axis=0)
    spectrum_upstream = jnp.fft.fft(upstream, n=padded, axis=0)
    conv_part = jnp.real(jnp.fft.ifft(spectrum_filter * spectrum_gated, axis=0))[:tokens]
    response = conv_part * scaling + skip * gated
    back_part = jnp.real(jnp.fft.ifft(jnp.conj(spectrum_filter) * spectrum_upstream, axis=0))[:tokens]
    back_signal = back_part * scaling + skip * upstream
    filter_part = jnp.real(jnp.fft.ifft(jnp.conj(spectrum_gated) * spectrum_upstream, axis=0))[:tokens]
    grad_filter = filter_part * scaling
    return (cotangent * response, back_signal * values, back_signal * keys, grad_filter)
```

```python
import math

import jax
import jax.numpy as jnp
import numpy as np
from jax import lax
from jax.experimental import pallas as pl
from jax.experimental.pallas import tpu as pltpu
from jax.sharding import PartitionSpec as P

DEVICES = 128
BLOCK = 256
LENGTH = DEVICES * BLOCK
HALF = 128
ROWS = 6
LOGICAL = pl.DeviceIdType.LOGICAL
bfloat16 = jnp.bfloat16


def tables():
    s = np.arange(DEVICES, dtype=np.float64)
    r = np.arange(BLOCK, dtype=np.float64)
    outer = np.exp(-2j * np.pi * np.outer(s + 0.25, s) / DEVICES)
    turn = np.exp(-2j * np.pi * np.outer(s + 0.25, r) / LENGTH)
    inner = np.exp(-2j * np.pi * (np.outer(r, r) % BLOCK) / BLOCK)
    scale = 1.0 / (LENGTH * math.sqrt(LENGTH))
    spread = np.concatenate([outer.real, outer.imag], 0)
    gather = np.concatenate([outer.real.T, outer.imag.T], 1) * scale
    inners = np.concatenate([inner.real, inner.imag], 1)
    turns = np.concatenate([turn.real, turn.imag], 0)
    return tuple(table.astype(np.float32) for table in (spread, gather, inners, turns))


def hops(offset):
    ring = (0, 1, 2, 1)
    return ring[(offset >> 1) & 3] + ring[(offset >> 3) & 3] + ring[(offset >> 5) & 3]


ORDER = sorted(range(1, DEVICES), key=lambda offset: -hops(offset))


def split(x):
    high = x.astype(bfloat16)
    low = (x - high.astype(jnp.float32)).astype(bfloat16)
    return high, low


def dot(a, b):
    return jnp.dot(a, b, preferred_element_type=jnp.float32)


def exchange_kernel(
    q_hbm, k_hbm, v_hbm, c_hbm, f_hbm, spread_hbm, gather_hbm, inners_hbm, turns_hbm,
    forward_out, back_out, filter_out,
    ins, spread_table, gather_table, inners, turns, spread, gather, fh, fl, gh, gl, outgoing, arrived, results, returned,
    in_sem, const_sem, send_sem, recv_sem, own_sem,
):
    sa, sb = lax.axis_index("sa"), lax.axis_index("sb")
    me = sa * 16 + sb
    z, y = sa >> 1, ((sa & 1) << 1) | ((sb >> 1) & 1)
    x, core = sb >> 2, sb & 1
    z_part = [((z + d) & 3) << 5 for d in range(4)]
    y_part = [(((y + d) & 2) << 3) | (((y + d) & 1) << 1) for d in range(4)]
    x_part = [((x + d) & 3) << 2 for d in range(4)]
    core_part = [core, 1 - core]

    def peer(offset):
        return z_part[(offset >> 5) & 3] | y_part[(offset >> 3) & 3] | x_part[(offset >> 1) & 3] | core_part[offset & 1]

    barrier = pltpu.get_barrier_semaphore()
    for offset in ORDER:
        pl.semaphore_signal(barrier, 1, device_id=peer(offset), device_id_type=LOGICAL)
    loads = [
        pltpu.make_async_copy(ref, ins.at[i], in_sem.at[i]) for i, ref in enumerate((q_hbm, k_hbm, v_hbm, c_hbm, f_hbm))
    ]
    for load in loads:
        load.start()
    pairs = ((spread_hbm, spread_table), (gather_hbm, gather_table), (inners_hbm, inners), (turns_hbm, turns))
    constants = [pltpu.make_async_copy(a, b, const_sem.at[i]) for i, (a, b) in enumerate(pairs)]
    for load in constants:
        load.start()
    for load in loads:
        load.wait()
    signals = (ins[1] * ins[2], ins[4], ins[3] * ins[0])
    for number, signal in enumerate(signals):
        for half in range(2):
            outgoing[:, 2 * number + half, :] = signal[half * HALF : (half + 1) * HALF, :].T
    for load in constants:
        load.wait()
    for table, target in ((spread_table, spread), (gather_table, gather)):
        high, low = split(table[...])
        width = table.shape[1]
        target[:, :width] = high
        target[:, width : 2 * width] = high
        target[:, 2 * width :] = low
    real_high, real_low = split(inners[:, :BLOCK])
    imag_high, imag_low = split(inners[:, BLOCK:])
    for real, imag, forward, inverse in ((real_high, imag_high, fh, gh), (real_low, imag_low, fl, gl)):
        for table, right, left in ((forward, imag, -imag), (inverse, -imag, imag)):
            table[:BLOCK, :BLOCK] = real
            table[:BLOCK, BLOCK:] = right
            table[BLOCK:, :BLOCK] = left
            table[BLOCK:, BLOCK:] = real
    pl.semaphore_wait(barrier, DEVICES - 1)

    def exchange(source, target, phase):
        for offset in ORDER:
            other = peer(offset)
            pltpu.make_async_remote_copy(
                src_ref=source.at[other, pl.ds(0, ROWS)],
                dst_ref=target.at[me, pl.ds(0, ROWS)],
                send_sem=send_sem.at[phase],
                recv_sem=recv_sem.at[phase],
                device_id=other,
                device_id_type=LOGICAL,
            ).start()
        own = pltpu.make_async_copy(
            source.at[me, pl.ds(0, ROWS)], target.at[me, pl.ds(0, ROWS)], own_sem.at[phase]
        )
        own.start()
        own.wait()
        landed = target.at[pl.ds(0, DEVICES - 1), pl.ds(0, ROWS)]
        pltpu.make_async_copy(landed, landed, recv_sem.at[phase]).wait()

    exchange(outgoing, arrived, 0)

    signal = jnp.concatenate([arrived[:, row, :] for row in range(ROWS)], 1)
    high, low = split(signal)
    first = dot(spread[...], jnp.concatenate([high, low, high], 0))
    turn_real, turn_imag = turns[:HALF, :], turns[HALF:, :]
    turned = []
    for number in range(3):
        real = first[:HALF, number * BLOCK : (number + 1) * BLOCK]
        imag = first[HALF:, number * BLOCK : (number + 1) * BLOCK]
        turned.append(
            jnp.concatenate([real * turn_real - imag * turn_imag, real * turn_imag + imag * turn_real], 1)
        )
    high, low = split(jnp.concatenate(turned, 0))
    spectra = dot(high, fh[...]) + dot(low, fh[...]) + dot(high, fl[...])
    gr, gi = spectra[:HALF, :BLOCK], spectra[:HALF, BLOCK:]
    fr, fi = spectra[HALF : 2 * HALF, :BLOCK], spectra[HALF : 2 * HALF, BLOCK:]
    ur, ui = spectra[2 * HALF :, :BLOCK], spectra[2 * HALF :, BLOCK:]
    products = (
        jnp.concatenate([fr * gr - fi * gi, fr * gi + fi * gr], 1),
        jnp.concatenate([fr * ur + fi * ui, fr * ui - fi * ur], 1),
        jnp.concatenate([gr * ur + gi * ui, gr * ui - gi * ur], 1),
    )
    high, low = split(jnp.concatenate(products, 0))
    second = dot(high, gh[...]) + dot(low, gh[...]) + dot(high, gl[...])
    turned = []
    for number in range(3):
        real = second[number * HALF : (number + 1) * HALF, :BLOCK]
        imag = second[number * HALF : (number + 1) * HALF, BLOCK:]
        turned.append(
            jnp.concatenate([real * turn_real + imag * turn_imag, imag * turn_real - real * turn_imag], 0)
        )
    high, low = split(jnp.concatenate(turned, 1))
    convolved = dot(gather[...], jnp.concatenate([high, low, high], 0))
    for row in range(ROWS):
        results[:, row, :] = convolved[:, row * HALF : (row + 1) * HALF]

    exchange(results, returned, 1)
    for number, out in enumerate((forward_out, back_out, filter_out)):
        for half in range(2):
            out[half * HALF : (half + 1) * HALF, :] = returned[:, 2 * number + half, :].T
    for phase, source in enumerate((outgoing, results)):
        sent = source.at[pl.ds(0, DEVICES - 1), pl.ds(0, ROWS)]
        pltpu.make_async_copy(sent, sent, send_sem.at[phase]).wait()


def local(queries, keys, values, cotangent, filt, skip):
    constants = tables()
    block = jax.ShapeDtypeStruct((BLOCK, DEVICES), jnp.float32)
    buffer = pltpu.VMEM((DEVICES, 8, HALF), jnp.float32)
    forward_conv, back_conv, filter_conv = pl.pallas_call(
        exchange_kernel,
        out_shape=(block, block, block),
        in_specs=[pl.BlockSpec(memory_space=pl.ANY)] * 9,
        out_specs=[pl.BlockSpec(memory_space=pltpu.VMEM)] * 3,
        scratch_shapes=[
            pltpu.VMEM((5, BLOCK, DEVICES), jnp.float32),
            *[pltpu.VMEM(c.shape, jnp.float32) for c in constants],
            pltpu.VMEM((BLOCK, 3 * DEVICES), bfloat16),
            pltpu.VMEM((DEVICES, 3 * BLOCK), bfloat16),
            *[pltpu.VMEM((2 * BLOCK, 2 * BLOCK), bfloat16)] * 4,
            buffer, buffer, buffer, buffer,
            pltpu.SemaphoreType.DMA((5,)),
            pltpu.SemaphoreType.DMA((4,)),
            pltpu.SemaphoreType.DMA((2,)),
            pltpu.SemaphoreType.DMA((2,)),
            pltpu.SemaphoreType.DMA((2,)),
        ],
        compiler_params=pltpu.CompilerParams(
            collective_id=0, has_side_effects=True, vmem_limit_bytes=60 * 1024 * 1024
        ),
        name="channel_convolutions",
    )(queries, keys, values, cotangent, filt, *[jnp.asarray(c) for c in constants])
    response = forward_conv + skip * (keys * values)
    back_signal = back_conv + skip * (cotangent * queries)
    return (cotangent * response, back_signal * values, back_signal * keys, filter_conv)


def solution(mesh):
    in_specs = (P(("sa", "sb"), None),) * 5 + (P(),)
    out_specs = (P(("sa", "sb"), None),) * 4
    return jax.shard_map(local, mesh=mesh, in_specs=in_specs, out_specs=out_specs, check_vma=False)
```

```python
import math

import jax
import jax.numpy as jnp
import numpy as np
from jax import lax
from jax.experimental import pallas as pl
from jax.experimental.pallas import tpu as pltpu
from jax.sharding import PartitionSpec as P

DEVICES = 128
BLOCK = 256
LENGTH = DEVICES * BLOCK
HALF = 128
ROWS = 6
LOGICAL = pl.DeviceIdType.LOGICAL
bfloat16 = jnp.bfloat16


def tables():
    s = np.arange(DEVICES, dtype=np.float64)
    r = np.arange(BLOCK, dtype=np.float64)
    outer = np.exp(-2j * np.pi * np.outer(s + 0.25, s) / DEVICES)
    turn = np.exp(-2j * np.pi * np.outer(s + 0.25, r) / LENGTH)
    inner = np.exp(-2j * np.pi * (np.outer(r, r) % BLOCK) / BLOCK)
    scale = 1.0 / (LENGTH * math.sqrt(LENGTH))
    spread = np.concatenate([outer.real, outer.imag], 0)
    gather = np.concatenate([outer.real.T, outer.imag.T], 1) * scale
    inners = np.concatenate([inner.real, inner.imag], 1)
    turns = np.concatenate([turn.real, turn.imag], 0)
    return tuple(table.astype(np.float32) for table in (spread, gather, inners, turns))


def hops(offset):
    ring = (0, 1, 2, 1)
    return ring[(offset >> 1) & 3] + ring[(offset >> 3) & 3] + ring[(offset >> 5) & 3]


ORDER = sorted(range(1, DEVICES), key=lambda offset: -hops(offset))
NEAR = [offset for offset in ORDER if hops(offset) <= 3]
FAR = [offset for offset in ORDER if hops(offset) > 3]
RELAYS = (0b0101010, 0b1111110)


def split(x):
    high = x.astype(bfloat16)
    low = (x - high.astype(jnp.float32)).astype(bfloat16)
    return high, low


def dot(a, b):
    return jnp.dot(a, b, preferred_element_type=jnp.float32)


def exchange_kernel(
    q_hbm, k_hbm, v_hbm, c_hbm, f_hbm, skip_hbm, spread_hbm, gather_hbm, inners_hbm, turns_hbm,
    returned, ins,
    skip, spread_table, gather_table, inners, turns, spread, gather, fh, fl, gh, gl, outgoing, arrived, results,
    in_sem, const_sem, send_sem, recv_sem, own_sem, relay_sem,
):
    sa, sb = lax.axis_index("sa"), lax.axis_index("sb")
    me = sa * 16 + sb
    z, y = sa >> 1, ((sa & 1) << 1) | ((sb >> 1) & 1)
    x, core = sb >> 2, sb & 1
    z_part = [((z + d) & 3) << 5 for d in range(4)]
    y_part = [(((y + d) & 2) << 3) | (((y + d) & 1) << 1) for d in range(4)]
    x_part = [((x + d) & 3) << 2 for d in range(4)]
    core_part = [core, 1 - core]

    def peer(offset):
        return z_part[(offset >> 5) & 3] | y_part[(offset >> 3) & 3] | x_part[(offset >> 1) & 3] | core_part[offset & 1]

    loads = [
        pltpu.make_async_copy(ref, ins.at[i], in_sem.at[i]) for i, ref in enumerate((q_hbm, k_hbm, v_hbm, c_hbm, f_hbm))
    ]
    loads.append(pltpu.make_async_copy(skip_hbm, skip, in_sem.at[5]))
    for load in loads:
        load.start()
    barrier = pltpu.get_barrier_semaphore()
    for offset in NEAR:
        pl.semaphore_signal(barrier, 1, device_id=peer(offset), device_id_type=LOGICAL)
    pairs = ((spread_hbm, spread_table), (gather_hbm, gather_table), (inners_hbm, inners), (turns_hbm, turns))
    constants = [pltpu.make_async_copy(a, b, const_sem.at[i]) for i, (a, b) in enumerate(pairs)]
    for load in constants:
        load.start()
    for load in loads:
        load.wait()
    gated, upstream = ins[1] * ins[2], ins[3] * ins[0]
    for number, signal in enumerate((gated, ins[4], upstream)):
        for half in range(2):
            outgoing[:, 2 * number + half, :] = signal[half * HALF : (half + 1) * HALF, :].T
    pl.semaphore_wait(barrier, len(NEAR))
    for offset in RELAYS:
        pl.semaphore_signal(relay_sem, 1, device_id=peer(offset), device_id_type=LOGICAL)

    def send(source, target, phase, offsets):
        for offset in offsets:
            other = peer(offset)
            pltpu.make_async_remote_copy(
                src_ref=source.at[other, pl.ds(0, ROWS)],
                dst_ref=target.at[me, pl.ds(0, ROWS)],
                send_sem=send_sem.at[phase],
                recv_sem=recv_sem.at[phase],
                device_id=other,
                device_id_type=LOGICAL,
            ).start()

    def receive(source, target, phase):
        own = pltpu.make_async_copy(
            source.at[me, pl.ds(0, ROWS)], target.at[me, pl.ds(0, ROWS)], own_sem.at[phase]
        )
        own.start()
        own.wait()
        landed = target.at[pl.ds(0, DEVICES - 1), pl.ds(0, ROWS)]
        pltpu.make_async_copy(landed, landed, recv_sem.at[phase]).wait()

    send(outgoing, arrived, 0, NEAR)
    pl.semaphore_wait(relay_sem, len(RELAYS))
    send(outgoing, arrived, 0, FAR)

    ins[0] = skip[...][None, :] * upstream
    ins[4] = skip[...][None, :] * gated
    for load in constants:
        load.wait()
    for table, target in ((spread_table, spread), (gather_table, gather)):
        high, low = split(table[...])
        width = table.shape[1]
        target[:, :width] = high
        target[:, width : 2 * width] = high
        target[:, 2 * width :] = low
    real_high, real_low = split(inners[:, :BLOCK])
    imag_high, imag_low = split(inners[:, BLOCK:])
    for real, imag, forward, inverse in ((real_high, imag_high, fh, gh), (real_low, imag_low, fl, gl)):
        for table, right, left in ((forward, imag, -imag), (inverse, -imag, imag)):
            table[:BLOCK, :BLOCK] = real
            table[:BLOCK, BLOCK:] = right
            table[BLOCK:, :BLOCK] = left
            table[BLOCK:, BLOCK:] = real
    receive(outgoing, arrived, 0)

    signal = jnp.concatenate([arrived[:, row, :] for row in range(ROWS)], 1)
    high, low = split(signal)
    first = dot(spread[...], jnp.concatenate([high, low, high], 0))
    turn_real, turn_imag = turns[:HALF, :], turns[HALF:, :]
    turned = []
    for number in range(3):
        real = first[:HALF, number * BLOCK : (number + 1) * BLOCK]
        imag = first[HALF:, number * BLOCK : (number + 1) * BLOCK]
        turned.append(
            jnp.concatenate([real * turn_real - imag * turn_imag, real * turn_imag + imag * turn_real], 1)
        )
    high, low = split(jnp.concatenate(turned, 0))
    spectra = dot(high, fh[...]) + dot(low, fh[...]) + dot(high, fl[...])
    gr, gi = spectra[:HALF, :BLOCK], spectra[:HALF, BLOCK:]
    fr, fi = spectra[HALF : 2 * HALF, :BLOCK], spectra[HALF : 2 * HALF, BLOCK:]
    ur, ui = spectra[2 * HALF :, :BLOCK], spectra[2 * HALF :, BLOCK:]
    products = (
        jnp.concatenate([fr * gr - fi * gi, fr * gi + fi * gr], 1),
        jnp.concatenate([fr * ur + fi * ui, fr * ui - fi * ur], 1),
        jnp.concatenate([gr * ur + gi * ui, gr * ui - gi * ur], 1),
    )
    high, low = split(jnp.concatenate(products, 0))
    second = dot(high, gh[...]) + dot(low, gh[...]) + dot(high, gl[...])
    turned = []
    for number in range(3):
        real = second[number * HALF : (number + 1) * HALF, :BLOCK]
        imag = second[number * HALF : (number + 1) * HALF, BLOCK:]
        turned.append(
            jnp.concatenate([real * turn_real + imag * turn_imag, imag * turn_real - real * turn_imag], 0)
        )
    high, low = split(jnp.concatenate(turned, 1))
    convolved = dot(gather[...], jnp.concatenate([high, low, high], 0))
    for row in range(ROWS):
        results[:, row, :] = convolved[:, row * HALF : (row + 1) * HALF]

    send(results, returned, 1, ORDER)
    receive(results, returned, 1)
    for phase, source in enumerate((outgoing, results)):
        sent = source.at[pl.ds(0, DEVICES - 1), pl.ds(0, ROWS)]
        pltpu.make_async_copy(sent, sent, send_sem.at[phase]).wait()


def finish_kernel(returned, ins, gq_hbm, gk_hbm, gv_hbm, gf_hbm, outs, sems):
    copies = []
    for half in range(2):
        rows = pl.ds(half * HALF, HALF)
        response = returned[:, half, :].T + ins[4, rows, :]
        back_signal = returned[:, 2 + half, :].T + ins[0, rows, :]
        outs[0, rows, :] = ins[3, rows, :] * response
        outs[1, rows, :] = back_signal * ins[2, rows, :]
        outs[2, rows, :] = back_signal * ins[1, rows, :]
        outs[3, rows, :] = returned[:, 4 + half, :].T
        for i, out in enumerate((gq_hbm, gk_hbm, gv_hbm, gf_hbm)):
            copies.append(pltpu.make_async_copy(outs.at[i, rows], out.at[rows], sems.at[i, half]))
            copies[-1].start()
    for copy in copies:
        copy.wait()


def local(queries, keys, values, cotangent, filt, skip):
    constants = tables()
    buffer = jax.ShapeDtypeStruct((DEVICES, 8, HALF), jnp.float32)
    block = jax.ShapeDtypeStruct((BLOCK, DEVICES), jnp.float32)
    five = jax.ShapeDtypeStruct((5, BLOCK, DEVICES), jnp.float32)
    returned, kept = pl.pallas_call(
        exchange_kernel,
        out_shape=(buffer, five),
        in_specs=[pl.BlockSpec(memory_space=pltpu.HBM)] * 10,
        out_specs=[pl.BlockSpec(memory_space=pltpu.VMEM)] * 2,
        scratch_shapes=[
            pltpu.VMEM((DEVICES,), jnp.float32),
            *[pltpu.VMEM(c.shape, jnp.float32) for c in constants],
            pltpu.VMEM((BLOCK, 3 * DEVICES), bfloat16),
            pltpu.VMEM((DEVICES, 3 * BLOCK), bfloat16),
            *[pltpu.VMEM((2 * BLOCK, 2 * BLOCK), bfloat16)] * 4,
            *[pltpu.VMEM(buffer.shape, buffer.dtype)] * 3,
            pltpu.SemaphoreType.DMA((6,)),
            pltpu.SemaphoreType.DMA((4,)),
            pltpu.SemaphoreType.DMA((2,)),
            pltpu.SemaphoreType.DMA((2,)),
            pltpu.SemaphoreType.DMA((2,)),
            pltpu.SemaphoreType.REGULAR,
        ],
        compiler_params=pltpu.CompilerParams(
            collective_id=0, has_side_effects=True, vmem_limit_bytes=40 * 1024 * 1024
        ),
        name="channel_convolutions",
    )(*[
        pltpu.with_memory_space_constraint(operand, pltpu.HBM)
        for operand in (queries, keys, values, cotangent, filt, skip, *map(jnp.asarray, constants))
    ])
    return pl.pallas_call(
        finish_kernel,
        out_shape=(block,) * 4,
        in_specs=[pl.BlockSpec(memory_space=pltpu.VMEM)] * 2,
        out_specs=[pl.BlockSpec(memory_space=pltpu.HBM)] * 4,
        scratch_shapes=[pltpu.VMEM((4, BLOCK, DEVICES), jnp.float32), pltpu.SemaphoreType.DMA((4, 2))],
        compiler_params=pltpu.CompilerParams(vmem_limit_bytes=8 * 1024 * 1024),
        name="gates",
    )(returned, kept)


def solution(mesh):
    in_specs = (P(("sa", "sb"), None),) * 5 + (P(),)
    out_specs = (P(("sa", "sb"), None),) * 4
    return jax.shard_map(local, mesh=mesh, in_specs=in_specs, out_specs=out_specs, check_vma=False)
```

```python
import math

import jax
import jax.numpy as jnp
import numpy as np
from jax import lax
from jax.experimental import pallas as pl
from jax.experimental.pallas import tpu as pltpu
from jax.sharding import PartitionSpec as P

DEVICES = 128
BLOCK = 256
LENGTH = DEVICES * BLOCK
HALF = 128
ROWS = 6
LOGICAL = pl.DeviceIdType.LOGICAL
bfloat16 = jnp.bfloat16
RING = (0, 1, 2, 1)
BEHIND = (0.0, 2.0, 2.5, 2.9), (0.0, 0.8, 1.1, 1.0)

def tables():
    s = np.arange(DEVICES, dtype=np.float64)
    r = np.arange(BLOCK, dtype=np.float64)
    half = r[:HALF]
    outer = np.exp(-2j * np.pi * np.outer(s + 0.25, s) / DEVICES)
    turn = np.exp(-2j * np.pi * np.outer(s + 0.25, r) / LENGTH)
    inner = np.exp(-2j * np.pi * (np.outer(half, half) % HALF) / HALF)
    twist = np.exp(-2j * np.pi * half / BLOCK)
    scale = 1.0 / (LENGTH * math.sqrt(LENGTH))
    spread = np.concatenate([outer.real, outer.imag], 0)
    gather = np.concatenate([outer.real.T, outer.imag.T], 1) * scale
    inners = np.concatenate([inner.real, inner.imag], 1)
    turns = np.concatenate([turn.real, turn.imag], 0)
    twists = np.zeros((8, HALF))
    twists[0], twists[1] = twist.real, twist.imag
    return tuple(table.astype(np.float32) for table in (spread, gather, inners, turns, twists))


def hops(offset):
    return RING[(offset >> 1) & 3] + RING[(offset >> 3) & 3] + RING[(offset >> 5) & 3]


def returns():
    places = [(z, y, x, c) for z in range(4) for y in range(4) for x in range(4) for c in (1, 0)]
    return sorted(places, key=lambda p: (BEHIND[0][p[0]] + BEHIND[1][p[2]] - 0.64 * RING[p[1]], -p[3]))


ORDER = sorted(range(1, DEVICES), key=lambda offset: (-hops(offset), (offset * 77) % DEVICES))


def split(x):
    high = x.astype(bfloat16)
    low = (x - high.astype(jnp.float32)).astype(bfloat16)
    return high, low


def dot(a, b):
    return jnp.dot(a, b, preferred_element_type=jnp.float32)


def product(a, b, conjugate):
    ar, ai, br, bi = a[:, :HALF], a[:, HALF:], b[:, :HALF], b[:, HALF:]
    if conjugate:
        return jnp.concatenate([ar * br + ai * bi, ar * bi - ai * br], 1)
    return jnp.concatenate([ar * br - ai * bi, ar * bi + ai * br], 1)


def exchange_kernel(
    q_hbm, k_hbm, v_hbm, c_hbm, f_hbm, skip_hbm, spread_hbm, gather_hbm, inners_hbm, turns_hbm, twists_hbm,
    returned, ins,
    skip, spread_table, gather_table, inners, turns, twists, spread, gather, forward, inverse,
    outgoing, arrived, results,
    in_sem, const_sem, send_sem, recv_sem, own_sem,
):
    sa, sb = lax.axis_index("sa"), lax.axis_index("sb")
    me = sa * 16 + sb
    z, y = sa >> 1, ((sa & 1) << 1) | ((sb >> 1) & 1)
    x, core = sb >> 2, sb & 1
    sign = 1 - 2 * core
    z_steps = [((z + sign * d) & 3) << 5 for d in range(4)]
    y_steps = [(((y + sign * d) & 2) << 3) | (((y + sign * d) & 1) << 1) for d in range(4)]
    x_steps = [((x + sign * d) & 3) << 2 for d in range(4)]
    cores = [core, 1 - core]

    def peer(offset):
        return z_steps[(offset >> 5) & 3] | y_steps[(offset >> 3) & 3] | x_steps[(offset >> 1) & 3] | cores[offset & 1]

    loads = [
        pltpu.make_async_copy(ref, ins.at[i], in_sem.at[i]) for i, ref in enumerate((q_hbm, k_hbm, v_hbm, c_hbm, f_hbm))
    ]
    loads.append(pltpu.make_async_copy(skip_hbm, skip, in_sem.at[5]))
    for load in loads:
        load.start()
    barrier = pltpu.get_barrier_semaphore()
    for offset in ORDER:
        pl.semaphore_signal(barrier, 1, device_id=peer(offset), device_id_type=LOGICAL)
    pairs = (
        (spread_hbm, spread_table), (gather_hbm, gather_table), (inners_hbm, inners), (turns_hbm, turns),
        (twists_hbm, twists),
    )
    constants = [pltpu.make_async_copy(a, b, const_sem.at[i]) for i, (a, b) in enumerate(pairs)]
    for load in constants:
        load.start()
    for load in loads:
        load.wait()
    gated, upstream = ins[1] * ins[2], ins[3] * ins[0]
    for number, signal in enumerate((gated, ins[4], upstream)):
        for half in range(2):
            outgoing[:, 2 * number + half, :] = signal[half * HALF : (half + 1) * HALF, :].T
    ins[0] = skip[...][None, :] * upstream
    ins[4] = skip[...][None, :] * gated

    for load in constants:
        load.wait()
    for table, target in ((spread_table, spread), (gather_table, gather)):
        high, low = split(table[...])
        width = table.shape[1]
        target[:, :width] = high
        target[:, width : 2 * width] = high
        target[:, 2 * width :] = low
    real_high, real_low = split(inners[:, :HALF])
    imag_high, imag_low = split(inners[:, HALF:])
    for base, real, imag in ((0, real_high, imag_high), (BLOCK, real_high, imag_high), (2 * BLOCK, real_low, imag_low)):
        for table, right, left in ((forward, imag, -imag), (inverse, -imag, imag)):
            table[base : base + HALF, :HALF] = real
            table[base : base + HALF, HALF:] = right
            table[base + HALF : base + BLOCK, :HALF] = left
            table[base + HALF : base + BLOCK, HALF:] = real

    def send(source, target, phase, other):
        pltpu.make_async_remote_copy(
            src_ref=source.at[other],
            dst_ref=target.at[me],
            send_sem=send_sem.at[phase],
            recv_sem=recv_sem.at[phase],
            device_id=other,
            device_id_type=LOGICAL,
        ).start()

    def receive(source, target, phase):
        own = pltpu.make_async_copy(source.at[me], target.at[me], own_sem.at[phase])
        own.start()
        own.wait()
        landed = target.at[pl.ds(0, DEVICES - 1)]
        pltpu.make_async_copy(landed, landed, recv_sem.at[phase]).wait()

    pl.semaphore_wait(barrier, DEVICES - 1)
    for offset in ORDER:
        send(outgoing, arrived, 0, peer(offset))
    receive(outgoing, arrived, 0)

    turn_real, turn_imag = turns[:HALF, :], turns[HALF:, :]
    twist_real, twist_imag = twists[0:1, :], twists[1:2, :]
    high, low = split(jnp.concatenate([arrived[:, row, :] for row in range(ROWS)], 1))
    first = dot(spread[...], jnp.concatenate([high, low, high], 0))
    parts = []
    for number in range(3):
        columns = slice(number * BLOCK, (number + 1) * BLOCK)
        real, imag = first[:HALF, columns], first[HALF:, columns]
        real, imag = real * turn_real - imag * turn_imag, real * turn_imag + imag * turn_real
        parts.append(jnp.concatenate([real[:, :HALF] + real[:, HALF:], imag[:, :HALF] + imag[:, HALF:]], 1))
        real, imag = real[:, :HALF] - real[:, HALF:], imag[:, :HALF] - imag[:, HALF:]
        parts.append(jnp.concatenate([real * twist_real - imag * twist_imag, real * twist_imag + imag * twist_real], 1))
    high, low = split(jnp.concatenate(parts, 0))
    spectra = dot(jnp.concatenate([high, low, high], 1), forward[...])
    gated_part, filter_part, upstream_part = (spectra[i * BLOCK : (i + 1) * BLOCK, :] for i in range(3))
    products = (
        product(filter_part, gated_part, False),
        product(filter_part, upstream_part, True),
        product(gated_part, upstream_part, True),
    )
    high, low = split(jnp.concatenate(products, 0))
    first = dot(jnp.concatenate([high, low, high], 1), inverse[...])
    parts = []
    for number in range(3):
        even = first[number * BLOCK : number * BLOCK + HALF, :]
        odd = first[number * BLOCK + HALF : (number + 1) * BLOCK, :]
        real, imag = odd[:, :HALF], odd[:, HALF:]
        real, imag = real * twist_real + imag * twist_imag, imag * twist_real - real * twist_imag
        real = jnp.concatenate([even[:, :HALF] + real, even[:, :HALF] - real], 1)
        imag = jnp.concatenate([even[:, HALF:] + imag, even[:, HALF:] - imag], 1)
        parts.append(jnp.concatenate([real * turn_real + imag * turn_imag, imag * turn_real - real * turn_imag], 0))
    high, low = split(jnp.concatenate(parts, 1))
    convolved = dot(gather[...], jnp.concatenate([high, low, high], 0))
    for row in range(ROWS):
        results[:, row, :] = convolved[:, row * HALF : (row + 1) * HALF]

    for to_z, step_y, to_x, step_core in returns():
        other = (to_z << 5) | y_steps[step_y] | (to_x << 2) | cores[step_core]
        if step_y == 0 and step_core == 0:
            pl.when(other != me)(lambda other=other: send(results, returned, 1, other))
        else:
            send(results, returned, 1, other)
    receive(results, returned, 1)
    for phase, source in enumerate((outgoing, results)):
        sent = source.at[pl.ds(0, DEVICES - 1)]
        pltpu.make_async_copy(sent, sent, send_sem.at[phase]).wait()


def finish_kernel(returned, ins, gq_hbm, gk_hbm, gv_hbm, gf_hbm, outs, sems):
    copies = []
    for half in range(2):
        rows = pl.ds(half * HALF, HALF)
        response = returned[:, half, :].T + ins[4, rows, :]
        back_signal = returned[:, 2 + half, :].T + ins[0, rows, :]
        outs[0, rows, :] = ins[3, rows, :] * response
        outs[1, rows, :] = back_signal * ins[2, rows, :]
        outs[2, rows, :] = back_signal * ins[1, rows, :]
        outs[3, rows, :] = returned[:, 4 + half, :].T
        for i, out in enumerate((gq_hbm, gk_hbm, gv_hbm, gf_hbm)):
            copies.append(pltpu.make_async_copy(outs.at[i, rows], out.at[rows], sems.at[i, half]))
            copies[-1].start()
    for copy in copies:
        copy.wait()


def local(queries, keys, values, cotangent, filt, skip):
    constants = tables()
    buffer = (DEVICES, ROWS, HALF)
    block = jax.ShapeDtypeStruct((BLOCK, DEVICES), jnp.float32)
    operands = (queries, keys, values, cotangent, filt, skip, *map(jnp.asarray, constants))
    returned, kept = pl.pallas_call(
        exchange_kernel,
        out_shape=(
            jax.ShapeDtypeStruct(buffer, jnp.float32),
            jax.ShapeDtypeStruct((5, BLOCK, DEVICES), jnp.float32),
        ),
        in_specs=[pl.BlockSpec(memory_space=pltpu.HBM)] * len(operands),
        out_specs=[pl.BlockSpec(memory_space=pltpu.VMEM)] * 2,
        scratch_shapes=[
            pltpu.VMEM((DEVICES,), jnp.float32),
            *[pltpu.VMEM(c.shape, jnp.float32) for c in constants],
            pltpu.VMEM((BLOCK, 3 * DEVICES), bfloat16),
            pltpu.VMEM((DEVICES, 3 * BLOCK), bfloat16),
            pltpu.VMEM((3 * BLOCK, BLOCK), bfloat16),
            pltpu.VMEM((3 * BLOCK, BLOCK), bfloat16),
            *[pltpu.VMEM(buffer, jnp.float32)] * 3,
            pltpu.SemaphoreType.DMA((6,)),
            pltpu.SemaphoreType.DMA((len(constants),)),
            pltpu.SemaphoreType.DMA((2,)),
            pltpu.SemaphoreType.DMA((2,)),
            pltpu.SemaphoreType.DMA((2,)),
        ],
        compiler_params=pltpu.CompilerParams(
            collective_id=0, has_side_effects=True, vmem_limit_bytes=40 * 1024 * 1024
        ),
        name="channel_convolutions",
    )(*[pltpu.with_memory_space_constraint(operand, pltpu.HBM) for operand in operands])
    return pl.pallas_call(
        finish_kernel,
        out_shape=(block,) * 4,
        in_specs=[pl.BlockSpec(memory_space=pltpu.VMEM)] * 2,
        out_specs=[pl.BlockSpec(memory_space=pltpu.HBM)] * 4,
        scratch_shapes=[pltpu.VMEM((4, BLOCK, DEVICES), jnp.float32), pltpu.SemaphoreType.DMA((4, 2))],
        compiler_params=pltpu.CompilerParams(vmem_limit_bytes=8 * 1024 * 1024),
        name="gates",
    )(returned, kept)


def solution(mesh):
    in_specs = (P(("sa", "sb"), None),) * 5 + (P(),)
    out_specs = (P(("sa", "sb"), None),) * 4
    return jax.shard_map(local, mesh=mesh, in_specs=in_specs, out_specs=out_specs, check_vma=False)
```

```python
import math

import jax
import jax.numpy as jnp
import numpy as np
from jax import lax
from jax.experimental import pallas as pl
from jax.experimental.pallas import tpu as pltpu
from jax.sharding import PartitionSpec as P

DEVICES = 128
BLOCK = 256
LENGTH = DEVICES * BLOCK
HALF = 128
ROWS = 6
LOGICAL = pl.DeviceIdType.LOGICAL
bfloat16 = jnp.bfloat16
RING = (0, 1, 2, 1)
BEHIND = (0.0, 2.0, 2.5, 2.9), (0.0, 0.8, 1.1, 1.0)

def tables():
    s = np.arange(DEVICES, dtype=np.float64)
    r = np.arange(BLOCK, dtype=np.float64)
    half = r[:HALF]
    outer = np.exp(-2j * np.pi * np.outer(s + 0.25, s) / DEVICES)
    turn = np.exp(-2j * np.pi * np.outer(s + 0.25, r) / LENGTH)
    inner = np.exp(-2j * np.pi * (np.outer(half, half) % HALF) / HALF)
    twist = np.exp(-2j * np.pi * half / BLOCK)
    scale = 1.0 / (LENGTH * math.sqrt(LENGTH))
    spread = np.concatenate([outer.real, outer.imag], 0)
    gather = np.concatenate([outer.real.T, outer.imag.T], 1) * scale
    inners = np.concatenate([inner.real, inner.imag], 1)
    turns = np.concatenate([turn.real, turn.imag], 0)
    twists = np.zeros((8, HALF))
    twists[0], twists[1] = twist.real, twist.imag
    return tuple(table.astype(np.float32) for table in (spread, gather, inners, turns, twists))


def hops(offset):
    return RING[(offset >> 1) & 3] + RING[(offset >> 3) & 3] + RING[(offset >> 5) & 3]


def returns():
    places = [(z, y, x, c) for z in range(4) for y in range(4) for x in range(4) for c in (1, 0)]
    return sorted(places, key=lambda p: (BEHIND[0][p[0]] + BEHIND[1][p[2]] - 0.64 * RING[p[1]], -p[3]))


ORDER = sorted(range(1, DEVICES), key=lambda offset: (-hops(offset), (offset * 77) % DEVICES))


def split(x):
    high = x.astype(bfloat16)
    low = (x - high.astype(jnp.float32)).astype(bfloat16)
    return high, low


def dot(a, b):
    return jnp.dot(a, b, preferred_element_type=jnp.float32)


def product(a, b, conjugate):
    ar, ai, br, bi = a[:, :HALF], a[:, HALF:], b[:, :HALF], b[:, HALF:]
    if conjugate:
        return jnp.concatenate([ar * br + ai * bi, ar * bi - ai * br], 1)
    return jnp.concatenate([ar * br - ai * bi, ar * bi + ai * br], 1)


def exchange_kernel(
    q_hbm, k_hbm, v_hbm, c_hbm, f_hbm, skip_hbm, spread_hbm, gather_hbm, inners_hbm, turns_hbm, twists_hbm,
    returned, ins,
    skip, spread_table, gather_table, inners, turns, twists, spread, gather, forward, inverse,
    outgoing, arrived, results,
    in_sem, const_sem, send_sem, recv_sem, own_sem,
):
    sa, sb = lax.axis_index("sa"), lax.axis_index("sb")
    me = sa * 16 + sb
    z, y = sa >> 1, ((sa & 1) << 1) | ((sb >> 1) & 1)
    x, core = sb >> 2, sb & 1
    sign = 1 - 2 * core
    z_steps = [((z + sign * d) & 3) << 5 for d in range(4)]
    y_steps = [(((y + sign * d) & 2) << 3) | (((y + sign * d) & 1) << 1) for d in range(4)]
    x_steps = [((x + sign * d) & 3) << 2 for d in range(4)]
    cores = [core, 1 - core]

    def peer(offset):
        return z_steps[(offset >> 5) & 3] | y_steps[(offset >> 3) & 3] | x_steps[(offset >> 1) & 3] | cores[offset & 1]

    loads = [
        pltpu.make_async_copy(ref, ins.at[i], in_sem.at[i]) for i, ref in enumerate((q_hbm, k_hbm, v_hbm, c_hbm, f_hbm))
    ]
    loads.append(pltpu.make_async_copy(skip_hbm, skip, in_sem.at[5]))
    for load in loads:
        load.start()
    barrier = pltpu.get_barrier_semaphore()
    for offset in ORDER:
        pl.semaphore_signal(barrier, 1, device_id=peer(offset), device_id_type=LOGICAL)
    pairs = (
        (spread_hbm, spread_table), (gather_hbm, gather_table), (inners_hbm, inners), (turns_hbm, turns),
        (twists_hbm, twists),
    )
    constants = [pltpu.make_async_copy(a, b, const_sem.at[i]) for i, (a, b) in enumerate(pairs)]
    for load in constants:
        load.start()
    for load in loads:
        load.wait()
    gated, upstream = ins[1] * ins[2], ins[3] * ins[0]
    for number, signal in enumerate((gated, ins[4], upstream)):
        for half in range(2):
            outgoing[:, 2 * number + half, :] = signal[half * HALF : (half + 1) * HALF, :].T
    def send(source, target, phase, other):
        pltpu.make_async_remote_copy(
            src_ref=source.at[other],
            dst_ref=target.at[me],
            send_sem=send_sem.at[phase],
            recv_sem=recv_sem.at[phase],
            device_id=other,
            device_id_type=LOGICAL,
        ).start()

    def receive(source, target, phase):
        own = pltpu.make_async_copy(source.at[me], target.at[me], own_sem.at[phase])
        own.start()
        own.wait()
        landed = target.at[pl.ds(0, DEVICES - 1)]
        pltpu.make_async_copy(landed, landed, recv_sem.at[phase]).wait()

    pl.semaphore_wait(barrier, DEVICES - 1)
    for offset in ORDER:
        send(outgoing, arrived, 0, peer(offset))
    ins[0] = skip[...][None, :] * upstream
    ins[4] = skip[...][None, :] * gated

    for load in constants:
        load.wait()
    for table, target in ((spread_table, spread), (gather_table, gather)):
        high, low = split(table[...])
        width = table.shape[1]
        target[:, :width] = high
        target[:, width : 2 * width] = high
        target[:, 2 * width :] = low
    real_high, real_low = split(inners[:, :HALF])
    imag_high, imag_low = split(inners[:, HALF:])
    for base, real, imag in ((0, real_high, imag_high), (BLOCK, real_high, imag_high), (2 * BLOCK, real_low, imag_low)):
        for table, right, left in ((forward, imag, -imag), (inverse, -imag, imag)):
            table[base : base + HALF, :HALF] = real
            table[base : base + HALF, HALF:] = right
            table[base + HALF : base + BLOCK, :HALF] = left
            table[base + HALF : base + BLOCK, HALF:] = real

    receive(outgoing, arrived, 0)

    turn_real, turn_imag = turns[:HALF, :], turns[HALF:, :]
    twist_real, twist_imag = twists[0:1, :], twists[1:2, :]

    def along_blocks(matrix, x):
        high, low = split(x)
        return dot(matrix[...], jnp.concatenate([high, low, high], 0))

    def along_positions(x, matrix):
        high, low = split(x)
        return dot(jnp.concatenate([high, low, high], 1), matrix[...])

    def turned(first):
        real, imag = first[:HALF, :], first[HALF:, :]
        real, imag = real * turn_real - imag * turn_imag, real * turn_imag + imag * turn_real
        even = jnp.concatenate([real[:, :HALF] + real[:, HALF:], imag[:, :HALF] + imag[:, HALF:]], 1)
        real, imag = real[:, :HALF] - real[:, HALF:], imag[:, :HALF] - imag[:, HALF:]
        return even, jnp.concatenate([real * twist_real - imag * twist_imag, real * twist_imag + imag * twist_real], 1)

    def turned_back(even, odd):
        real, imag = odd[:, :HALF], odd[:, HALF:]
        real, imag = real * twist_real + imag * twist_imag, imag * twist_real - real * twist_imag
        real = jnp.concatenate([even[:, :HALF] + real, even[:, :HALF] - real], 1)
        imag = jnp.concatenate([even[:, HALF:] + imag, even[:, HALF:] - imag], 1)
        return jnp.concatenate([real * turn_real + imag * turn_imag, imag * turn_real - real * turn_imag], 0)

    firsts = [
        along_blocks(spread, jnp.concatenate([arrived[:, row, :], arrived[:, row + 1, :]], 1)) for row in (0, 2, 4)
    ]
    parts = [turned(first) for first in firsts]
    gated_part, filter_part, upstream_part = ([along_positions(half, forward) for half in part] for part in parts)
    products = [
        [product(a, b, conjugate) for a, b in zip(left, right)]
        for left, right, conjugate in (
            (filter_part, gated_part, False),
            (filter_part, upstream_part, True),
            (gated_part, upstream_part, True),
        )
    ]
    firsts = [[along_positions(half, inverse) for half in part] for part in products]
    parts = [turned_back(even, odd) for even, odd in firsts]
    for number, part in enumerate(parts):
        convolved = along_blocks(gather, part)
        for half in range(2):
            results[:, 2 * number + half, :] = convolved[:, half * HALF : (half + 1) * HALF]

    for to_z, step_y, to_x, step_core in returns():
        other = (to_z << 5) | y_steps[step_y] | (to_x << 2) | cores[step_core]
        if step_y == 0 and step_core == 0:
            pl.when(other != me)(lambda other=other: send(results, returned, 1, other))
        else:
            send(results, returned, 1, other)
    receive(results, returned, 1)
    for phase, source in enumerate((outgoing, results)):
        sent = source.at[pl.ds(0, DEVICES - 1)]
        pltpu.make_async_copy(sent, sent, send_sem.at[phase]).wait()


def finish_kernel(returned, ins, gq_hbm, gk_hbm, gv_hbm, gf_hbm, outs, sems):
    copies = []
    for half in range(2):
        rows = pl.ds(half * HALF, HALF)
        response = returned[:, half, :].T + ins[4, rows, :]
        back_signal = returned[:, 2 + half, :].T + ins[0, rows, :]
        outs[0, rows, :] = ins[3, rows, :] * response
        outs[1, rows, :] = back_signal * ins[2, rows, :]
        outs[2, rows, :] = back_signal * ins[1, rows, :]
        outs[3, rows, :] = returned[:, 4 + half, :].T
        for i, out in enumerate((gq_hbm, gk_hbm, gv_hbm, gf_hbm)):
            copies.append(pltpu.make_async_copy(outs.at[i, rows], out.at[rows], sems.at[i, half]))
            copies[-1].start()
    for copy in copies:
        copy.wait()


def local(queries, keys, values, cotangent, filt, skip):
    constants = tables()
    buffer = (DEVICES, ROWS, HALF)
    block = jax.ShapeDtypeStruct((BLOCK, DEVICES), jnp.float32)
    operands = (queries, keys, values, cotangent, filt, skip, *map(jnp.asarray, constants))
    returned, kept = pl.pallas_call(
        exchange_kernel,
        out_shape=(
            jax.ShapeDtypeStruct(buffer, jnp.float32),
            jax.ShapeDtypeStruct((5, BLOCK, DEVICES), jnp.float32),
        ),
        in_specs=[pl.BlockSpec(memory_space=pltpu.HBM)] * len(operands),
        out_specs=[pl.BlockSpec(memory_space=pltpu.VMEM)] * 2,
        scratch_shapes=[
            pltpu.VMEM((DEVICES,), jnp.float32),
            *[pltpu.VMEM(c.shape, jnp.float32) for c in constants],
            pltpu.VMEM((BLOCK, 3 * DEVICES), bfloat16),
            pltpu.VMEM((DEVICES, 3 * BLOCK), bfloat16),
            pltpu.VMEM((3 * BLOCK, BLOCK), bfloat16),
            pltpu.VMEM((3 * BLOCK, BLOCK), bfloat16),
            *[pltpu.VMEM(buffer, jnp.float32)] * 3,
            pltpu.SemaphoreType.DMA((6,)),
            pltpu.SemaphoreType.DMA((len(constants),)),
            pltpu.SemaphoreType.DMA((2,)),
            pltpu.SemaphoreType.DMA((2,)),
            pltpu.SemaphoreType.DMA((2,)),
        ],
        compiler_params=pltpu.CompilerParams(
            collective_id=0, has_side_effects=True, vmem_limit_bytes=40 * 1024 * 1024
        ),
        name="channel_convolutions",
    )(*[pltpu.with_memory_space_constraint(operand, pltpu.HBM) for operand in operands])
    return pl.pallas_call(
        finish_kernel,
        out_shape=(block,) * 4,
        in_specs=[pl.BlockSpec(memory_space=pltpu.VMEM)] * 2,
        out_specs=[pl.BlockSpec(memory_space=pltpu.HBM)] * 4,
        scratch_shapes=[pltpu.VMEM((4, BLOCK, DEVICES), jnp.float32), pltpu.SemaphoreType.DMA((4, 2))],
        compiler_params=pltpu.CompilerParams(vmem_limit_bytes=8 * 1024 * 1024),
        name="gates",
    )(returned, kept)


def solution(mesh):
    in_specs = (P(("sa", "sb"), None),) * 5 + (P(),)
    out_specs = (P(("sa", "sb"), None),) * 4
    return jax.shard_map(local, mesh=mesh, in_specs=in_specs, out_specs=out_specs, check_vma=False)
```

```python
import math

import jax
import jax.numpy as jnp
import numpy as np
from jax import lax
from jax.experimental import pallas as pl
from jax.experimental.pallas import tpu as pltpu
from jax.sharding import PartitionSpec as P

DEVICES = 128
BLOCK = 256
LENGTH = DEVICES * BLOCK
HALF = 128
ROWS = 6
LOGICAL = pl.DeviceIdType.LOGICAL
bfloat16 = jnp.bfloat16
RING = (0, 1, 2, 1)
BEHIND = (0.0, 2.0, 2.5, 2.9), (0.0, 0.8, 1.1, 1.0)

def tables():
    s = np.arange(DEVICES, dtype=np.float64)
    r = np.arange(BLOCK, dtype=np.float64)
    half = r[:HALF]
    outer = np.exp(-2j * np.pi * np.outer(s + 0.25, s) / DEVICES)
    turn = np.exp(-2j * np.pi * np.outer(s + 0.25, r) / LENGTH)
    inner = np.exp(-2j * np.pi * (np.outer(half, half) % HALF) / HALF)
    twist = np.exp(-2j * np.pi * half / BLOCK)
    scale = 1.0 / (LENGTH * math.sqrt(LENGTH))
    spread = np.concatenate([outer.real, outer.imag], 0)
    gather = np.concatenate([outer.real.T, outer.imag.T], 1) * scale
    inners = np.concatenate([inner.real, inner.imag], 1)
    turns = np.concatenate([turn.real, turn.imag], 0)
    twists = np.zeros((8, HALF))
    twists[0], twists[1] = twist.real, twist.imag
    return tuple(table.astype(np.float32) for table in (spread, gather, inners, turns, twists))


def hops(offset):
    return RING[(offset >> 1) & 3] + RING[(offset >> 3) & 3] + RING[(offset >> 5) & 3]


def returns():
    places = [(z, y, x, c) for z in range(4) for y in range(4) for x in range(4) for c in (1, 0)]
    return sorted(places, key=lambda p: (BEHIND[0][p[0]] + BEHIND[1][p[2]] - 0.64 * RING[p[1]], -p[3]))


ORDER = sorted(
    range(1, DEVICES),
    key=lambda s: (-(s >> 6), -RING[(s >> 3) & 3] - RING[(s >> 1) & 3] - 0.5 * ((s >> 5) & 1), (s * 77) % DEVICES),
)


def split(x):
    high = x.astype(bfloat16)
    low = (x - high.astype(jnp.float32)).astype(bfloat16)
    return high, low


def dot(a, b):
    return jnp.dot(a, b, preferred_element_type=jnp.float32)


def product(a, b, conjugate):
    ar, ai, br, bi = a[:, :HALF], a[:, HALF:], b[:, :HALF], b[:, HALF:]
    if conjugate:
        return jnp.concatenate([ar * br + ai * bi, ar * bi - ai * br], 1)
    return jnp.concatenate([ar * br - ai * bi, ar * bi + ai * br], 1)


def exchange_kernel(
    q_hbm, k_hbm, v_hbm, c_hbm, f_hbm, skip_hbm, spread_hbm, gather_hbm, inners_hbm, turns_hbm, twists_hbm,
    returned, ins,
    skip, spread_table, gather_table, inners, turns, twists, spread, gather, forward, inverse,
    outgoing, arrived, results,
    in_sem, const_sem, send_sem, recv_sem, own_sem,
):
    sa, sb = lax.axis_index("sa"), lax.axis_index("sb")
    me = sa * 16 + sb
    z, y = sa >> 1, ((sa & 1) << 1) | ((sb >> 1) & 1)
    x, core = sb >> 2, sb & 1
    sign = 1 - 2 * core
    z_steps = [(z ^ d) << 5 for d in range(4)]
    y_steps = [(((y + sign * d) & 2) << 3) | (((y + sign * d) & 1) << 1) for d in range(4)]
    x_steps = [((x + sign * d) & 3) << 2 for d in range(4)]
    cores = [core, 1 - core]

    def peer(offset):
        return z_steps[(offset >> 5) & 3] | y_steps[(offset >> 3) & 3] | x_steps[(offset >> 1) & 3] | cores[offset & 1]

    loads = [
        pltpu.make_async_copy(ref, ins.at[i], in_sem.at[i]) for i, ref in enumerate((q_hbm, k_hbm, v_hbm, c_hbm, f_hbm))
    ]
    loads.append(pltpu.make_async_copy(skip_hbm, skip, in_sem.at[5]))
    for load in loads:
        load.start()
    barrier = pltpu.get_barrier_semaphore()
    for offset in ORDER:
        pl.semaphore_signal(barrier, 1, device_id=peer(offset), device_id_type=LOGICAL)
    pairs = (
        (spread_hbm, spread_table), (gather_hbm, gather_table), (inners_hbm, inners), (turns_hbm, turns),
        (twists_hbm, twists),
    )
    constants = [pltpu.make_async_copy(a, b, const_sem.at[i]) for i, (a, b) in enumerate(pairs)]
    for load in constants:
        load.start()
    for load in loads:
        load.wait()
    gated, upstream = ins[1] * ins[2], ins[3] * ins[0]
    for number, signal in enumerate((gated, ins[4], upstream)):
        for half in range(2):
            outgoing[:, 2 * number + half, :] = signal[half * HALF : (half + 1) * HALF, :].T
    def send(source, target, phase, other):
        pltpu.make_async_remote_copy(
            src_ref=source.at[other],
            dst_ref=target.at[me],
            send_sem=send_sem.at[phase],
            recv_sem=recv_sem.at[phase],
            device_id=other,
            device_id_type=LOGICAL,
        ).start()

    def receive(source, target, phase):
        own = pltpu.make_async_copy(source.at[me], target.at[me], own_sem.at[phase])
        own.start()
        own.wait()
        landed = target.at[pl.ds(0, DEVICES - 1)]
        pltpu.make_async_copy(landed, landed, recv_sem.at[phase]).wait()

    pl.semaphore_wait(barrier, DEVICES - 1)
    for offset in ORDER:
        send(outgoing, arrived, 0, peer(offset))
    ins[0] = skip[...][None, :] * upstream
    ins[4] = skip[...][None, :] * gated

    for load in constants:
        load.wait()
    for table, target in ((spread_table, spread), (gather_table, gather)):
        high, low = split(table[...])
        width = table.shape[1]
        target[:, :width] = high
        target[:, width : 2 * width] = high
        target[:, 2 * width :] = low
    real_high, real_low = split(inners[:, :HALF])
    imag_high, imag_low = split(inners[:, HALF:])
    for base, real, imag in ((0, real_high, imag_high), (BLOCK, real_high, imag_high), (2 * BLOCK, real_low, imag_low)):
        for table, right, left in ((forward, imag, -imag), (inverse, -imag, imag)):
            table[base : base + HALF, :HALF] = real
            table[base : base + HALF, HALF:] = right
            table[base + HALF : base + BLOCK, :HALF] = left
            table[base + HALF : base + BLOCK, HALF:] = real

    receive(outgoing, arrived, 0)

    turn_real, turn_imag = turns[:HALF, :], turns[HALF:, :]
    twist_real, twist_imag = twists[0:1, :], twists[1:2, :]

    def along_blocks(matrix, x):
        high, low = split(x)
        return dot(matrix[...], jnp.concatenate([high, low, high], 0))

    def along_positions(x, matrix):
        high, low = split(x)
        return dot(jnp.concatenate([high, low, high], 1), matrix[...])

    def turned(first):
        real, imag = first[:HALF, :], first[HALF:, :]
        real, imag = real * turn_real - imag * turn_imag, real * turn_imag + imag * turn_real
        even = jnp.concatenate([real[:, :HALF] + real[:, HALF:], imag[:, :HALF] + imag[:, HALF:]], 1)
        real, imag = real[:, :HALF] - real[:, HALF:], imag[:, :HALF] - imag[:, HALF:]
        return even, jnp.concatenate([real * twist_real - imag * twist_imag, real * twist_imag + imag * twist_real], 1)

    def turned_back(even, odd):
        real, imag = odd[:, :HALF], odd[:, HALF:]
        real, imag = real * twist_real + imag * twist_imag, imag * twist_real - real * twist_imag
        real = jnp.concatenate([even[:, :HALF] + real, even[:, :HALF] - real], 1)
        imag = jnp.concatenate([even[:, HALF:] + imag, even[:, HALF:] - imag], 1)
        return jnp.concatenate([real * turn_real + imag * turn_imag, imag * turn_real - real * turn_imag], 0)

    firsts = [
        along_blocks(spread, jnp.concatenate([arrived[:, row, :], arrived[:, row + 1, :]], 1)) for row in (0, 2, 4)
    ]
    parts = [turned(first) for first in firsts]
    gated_part, filter_part, upstream_part = ([along_positions(half, forward) for half in part] for part in parts)
    products = [
        [product(a, b, conjugate) for a, b in zip(left, right)]
        for left, right, conjugate in (
            (filter_part, gated_part, False),
            (filter_part, upstream_part, True),
            (gated_part, upstream_part, True),
        )
    ]
    firsts = [[along_positions(half, inverse) for half in part] for part in products]
    parts = [turned_back(even, odd) for even, odd in firsts]
    for number, part in enumerate(parts):
        convolved = along_blocks(gather, part)
        for half in range(2):
            results[:, 2 * number + half, :] = convolved[:, half * HALF : (half + 1) * HALF]

    for to_z, step_y, to_x, step_core in returns():
        other = (to_z << 5) | y_steps[step_y] | (to_x << 2) | cores[step_core]
        if step_y == 0 and step_core == 0:
            pl.when(other != me)(lambda other=other: send(results, returned, 1, other))
        else:
            send(results, returned, 1, other)
    receive(results, returned, 1)
    for phase, source in enumerate((outgoing, results)):
        sent = source.at[pl.ds(0, DEVICES - 1)]
        pltpu.make_async_copy(sent, sent, send_sem.at[phase]).wait()


def finish_kernel(returned, ins, gq_hbm, gk_hbm, gv_hbm, gf_hbm, outs, sems):
    copies = []
    for half in range(2):
        rows = pl.ds(half * HALF, HALF)
        response = returned[:, half, :].T + ins[4, rows, :]
        back_signal = returned[:, 2 + half, :].T + ins[0, rows, :]
        outs[0, rows, :] = ins[3, rows, :] * response
        outs[1, rows, :] = back_signal * ins[2, rows, :]
        outs[2, rows, :] = back_signal * ins[1, rows, :]
        outs[3, rows, :] = returned[:, 4 + half, :].T
        for i, out in enumerate((gq_hbm, gk_hbm, gv_hbm, gf_hbm)):
            copies.append(pltpu.make_async_copy(outs.at[i, rows], out.at[rows], sems.at[i, half]))
            copies[-1].start()
    for copy in copies:
        copy.wait()


def local(queries, keys, values, cotangent, filt, skip):
    constants = tables()
    buffer = (DEVICES, ROWS, HALF)
    block = jax.ShapeDtypeStruct((BLOCK, DEVICES), jnp.float32)
    operands = (queries, keys, values, cotangent, filt, skip, *map(jnp.asarray, constants))
    returned, kept = pl.pallas_call(
        exchange_kernel,
        out_shape=(
            jax.ShapeDtypeStruct(buffer, jnp.float32),
            jax.ShapeDtypeStruct((5, BLOCK, DEVICES), jnp.float32),
        ),
        in_specs=[pl.BlockSpec(memory_space=pltpu.HBM)] * len(operands),
        out_specs=[pl.BlockSpec(memory_space=pltpu.VMEM)] * 2,
        scratch_shapes=[
            pltpu.VMEM((DEVICES,), jnp.float32),
            *[pltpu.VMEM(c.shape, jnp.float32) for c in constants],
            pltpu.VMEM((BLOCK, 3 * DEVICES), bfloat16),
            pltpu.VMEM((DEVICES, 3 * BLOCK), bfloat16),
            pltpu.VMEM((3 * BLOCK, BLOCK), bfloat16),
            pltpu.VMEM((3 * BLOCK, BLOCK), bfloat16),
            *[pltpu.VMEM(buffer, jnp.float32)] * 3,
            pltpu.SemaphoreType.DMA((6,)),
            pltpu.SemaphoreType.DMA((len(constants),)),
            pltpu.SemaphoreType.DMA((2,)),
            pltpu.SemaphoreType.DMA((2,)),
            pltpu.SemaphoreType.DMA((2,)),
        ],
        compiler_params=pltpu.CompilerParams(
            collective_id=0, has_side_effects=True, vmem_limit_bytes=40 * 1024 * 1024
        ),
        name="channel_convolutions",
    )(*[pltpu.with_memory_space_constraint(operand, pltpu.HBM) for operand in operands])
    return pl.pallas_call(
        finish_kernel,
        out_shape=(block,) * 4,
        in_specs=[pl.BlockSpec(memory_space=pltpu.VMEM)] * 2,
        out_specs=[pl.BlockSpec(memory_space=pltpu.HBM)] * 4,
        scratch_shapes=[pltpu.VMEM((4, BLOCK, DEVICES), jnp.float32), pltpu.SemaphoreType.DMA((4, 2))],
        compiler_params=pltpu.CompilerParams(vmem_limit_bytes=8 * 1024 * 1024),
        name="gates",
    )(returned, kept)


def solution(mesh):
    in_specs = (P(("sa", "sb"), None),) * 5 + (P(),)
    out_specs = (P(("sa", "sb"), None),) * 4
    return jax.shard_map(local, mesh=mesh, in_specs=in_specs, out_specs=out_specs, check_vma=False)
```

```python
import math

import jax
import jax.numpy as jnp
import numpy as np
from jax import lax
from jax.experimental import pallas as pl
from jax.experimental.pallas import tpu as pltpu
from jax.sharding import PartitionSpec as P

DEVICES = 128
BLOCK = 256
LENGTH = DEVICES * BLOCK
HALF = 128
ROWS = 6
LOGICAL = pl.DeviceIdType.LOGICAL
bfloat16 = jnp.bfloat16
RING = (0, 1, 2, 1)
BEHIND = (0.0, 2.0, 2.5, 2.9), (0.0, 0.8, 1.1, 1.0)

def tables():
    s = np.arange(DEVICES, dtype=np.float64)
    r = np.arange(BLOCK, dtype=np.float64)
    half = r[:HALF]
    outer = np.exp(-2j * np.pi * np.outer(s + 0.25, s) / DEVICES)
    turn = np.exp(-2j * np.pi * np.outer(s + 0.25, r) / LENGTH)
    inner = np.exp(-2j * np.pi * (np.outer(half, half) % HALF) / HALF)
    twist = np.exp(-2j * np.pi * half / BLOCK)
    scale = 1.0 / (LENGTH * math.sqrt(LENGTH))
    spread = np.concatenate([outer.real, outer.imag], 0)
    gather = np.concatenate([outer.real.T, outer.imag.T], 1) * scale
    inners = np.concatenate([inner.real, inner.imag], 1)
    turns = np.concatenate([turn.real, turn.imag], 0)
    twists = np.zeros((8, HALF))
    twists[0], twists[1] = twist.real, twist.imag
    return tuple(table.astype(np.float32) for table in (spread, gather, inners, turns, twists))


def hops(offset):
    return RING[(offset >> 1) & 3] + RING[(offset >> 3) & 3] + RING[(offset >> 5) & 3]


def returns():
    places = [(z, y, x, c) for z in range(4) for y in range(4) for x in range(4) for c in (1, 0)]
    return sorted(places, key=lambda p: (BEHIND[0][p[0]] + BEHIND[1][p[2]] - 0.64 * RING[p[1]], -p[3]))


ORDER = sorted(
    range(1, DEVICES),
    key=lambda s: (-(s >> 6), -RING[(s >> 3) & 3] - RING[(s >> 1) & 3] - 0.5 * ((s >> 5) & 1), (s * 77) % DEVICES),
)


def split(x):
    high = x.astype(bfloat16)
    low = (x - high.astype(jnp.float32)).astype(bfloat16)
    return high, low


def dot(a, b):
    return jnp.dot(a, b, preferred_element_type=jnp.float32)


def product(a, b, conjugate):
    ar, ai, br, bi = a[:, :HALF], a[:, HALF:], b[:, :HALF], b[:, HALF:]
    if conjugate:
        return jnp.concatenate([ar * br + ai * bi, ar * bi - ai * br], 1)
    return jnp.concatenate([ar * br - ai * bi, ar * bi + ai * br], 1)


def exchange_kernel(
    q_hbm, k_hbm, v_hbm, c_hbm, f_hbm, skip_hbm, spread_hbm, gather_hbm, inners_hbm, turns_hbm, twists_hbm,
    returned, ins,
    skip, spread_table, gather_table, inners, turns, twists, spread, gather, forward, inverse,
    outgoing, arrived, results,
    in_sem, const_sem, send_sem, recv_sem, own_sem,
):
    sa, sb = lax.axis_index("sa"), lax.axis_index("sb")
    me = sa * 16 + sb
    z, y = sa >> 1, ((sa & 1) << 1) | ((sb >> 1) & 1)
    x, core = sb >> 2, sb & 1
    sign = 1 - 2 * core
    z_steps = [(z ^ d) << 5 for d in range(4)]
    y_steps = [(((y + sign * d) & 2) << 3) | (((y + sign * d) & 1) << 1) for d in range(4)]
    x_steps = [((x + sign * d) & 3) << 2 for d in range(4)]
    cores = [core, 1 - core]

    def peer(offset):
        return z_steps[(offset >> 5) & 3] | y_steps[(offset >> 3) & 3] | x_steps[(offset >> 1) & 3] | cores[offset & 1]

    loads = [
        pltpu.make_async_copy(ref, ins.at[i], in_sem.at[i]) for i, ref in enumerate((q_hbm, k_hbm, v_hbm, c_hbm, f_hbm))
    ]
    loads.append(pltpu.make_async_copy(skip_hbm, skip, in_sem.at[5]))
    for load in loads:
        load.start()
    barrier = pltpu.get_barrier_semaphore()
    for offset in ORDER:
        pl.semaphore_signal(barrier, 1, device_id=peer(offset), device_id_type=LOGICAL)
    pairs = (
        (spread_hbm, spread_table), (gather_hbm, gather_table), (inners_hbm, inners), (turns_hbm, turns),
        (twists_hbm, twists),
    )
    constants = [pltpu.make_async_copy(a, b, const_sem.at[i]) for i, (a, b) in enumerate(pairs)]
    for load in constants:
        load.start()
    for load in loads:
        load.wait()
    gated, upstream = ins[1] * ins[2], ins[3] * ins[0]
    for number, signal in enumerate((gated, ins[4], upstream)):
        for half in range(2):
            outgoing[:, 2 * number + half, :] = signal[half * HALF : (half + 1) * HALF, :].T
    def send(source, target, phase, other):
        pltpu.make_async_remote_copy(
            src_ref=source.at[other],
            dst_ref=target.at[me],
            send_sem=send_sem.at[phase],
            recv_sem=recv_sem.at[phase],
            device_id=other,
            device_id_type=LOGICAL,
        ).start()

    def receive(source, target, phase):
        own = pltpu.make_async_copy(source.at[me], target.at[me], own_sem.at[phase])
        own.start()
        own.wait()
        landed = target.at[pl.ds(0, DEVICES - 1)]
        pltpu.make_async_copy(landed, landed, recv_sem.at[phase]).wait()

    pl.semaphore_wait(barrier, DEVICES - 1)
    for offset in ORDER:
        send(outgoing, arrived, 0, peer(offset))
    ins[0] = skip[...][None, :] * upstream
    ins[4] = skip[...][None, :] * gated

    for load in constants:
        load.wait()
    for table, target in ((spread_table, spread), (gather_table, gather)):
        high, low = split(table[...])
        width = table.shape[1]
        target[:, :width] = high
        target[:, width : 2 * width] = high
        target[:, 2 * width :] = low
    real_high, real_low = split(inners[:, :HALF])
    imag_high, imag_low = split(inners[:, HALF:])
    for base, real, imag in ((0, real_high, imag_high), (BLOCK, real_high, imag_high), (2 * BLOCK, real_low, imag_low)):
        for table, right, left in ((forward, imag, -imag), (inverse, -imag, imag)):
            table[base : base + HALF, :HALF] = real
            table[base : base + HALF, HALF:] = right
            table[base + HALF : base + BLOCK, :HALF] = left
            table[base + HALF : base + BLOCK, HALF:] = real

    receive(outgoing, arrived, 0)

    turn_real, turn_imag = turns[:HALF, :], turns[HALF:, :]
    twist_real, twist_imag = twists[0:1, :], twists[1:2, :]

    def along_blocks(matrix, x):
        high, low = split(x)
        return dot(matrix[...], jnp.concatenate([high, low, high], 0))

    def along_positions(x, matrix):
        high, low = split(x)
        return dot(jnp.concatenate([high, low, high], 1), matrix[...])

    def turned(first):
        real, imag = first[:HALF, :], first[HALF:, :]
        real, imag = real * turn_real - imag * turn_imag, real * turn_imag + imag * turn_real
        even = jnp.concatenate([real[:, :HALF] + real[:, HALF:], imag[:, :HALF] + imag[:, HALF:]], 1)
        real, imag = real[:, :HALF] - real[:, HALF:], imag[:, :HALF] - imag[:, HALF:]
        return even, jnp.concatenate([real * twist_real - imag * twist_imag, real * twist_imag + imag * twist_real], 1)

    def turned_back(even, odd):
        real, imag = odd[:, :HALF], odd[:, HALF:]
        real, imag = real * twist_real + imag * twist_imag, imag * twist_real - real * twist_imag
        real = jnp.concatenate([even[:, :HALF] + real, even[:, :HALF] - real], 1)
        imag = jnp.concatenate([even[:, HALF:] + imag, even[:, HALF:] - imag], 1)
        return jnp.concatenate([real * turn_real + imag * turn_imag, imag * turn_real - real * turn_imag], 0)

    firsts = [
        along_blocks(spread, jnp.concatenate([arrived[:, row, :], arrived[:, row + 1, :]], 1)) for row in (0, 2, 4)
    ]
    parts = [turned(first) for first in firsts]
    gated_part, filter_part, upstream_part = ([along_positions(half, forward) for half in part] for part in parts)
    products = [
        [product(a, b, conjugate) for a, b in zip(left, right)]
        for left, right, conjugate in (
            (filter_part, gated_part, False),
            (filter_part, upstream_part, True),
            (gated_part, upstream_part, True),
        )
    ]
    firsts = [[along_positions(half, inverse) for half in part] for part in products]
    parts = [turned_back(even, odd) for even, odd in firsts]
    for number, part in enumerate(parts):
        convolved = along_blocks(gather, part)
        for half in range(2):
            results[:, 2 * number + half, :] = convolved[:, half * HALF : (half + 1) * HALF]

    for to_z, step_y, to_x, step_core in returns():
        other = (to_z << 5) | y_steps[step_y] | (to_x << 2) | cores[step_core]
        if step_y == 0 and step_core == 0:
            pl.when(other != me)(lambda other=other: send(results, returned, 1, other))
        else:
            send(results, returned, 1, other)
    for phase, source in enumerate((outgoing, results)):
        sent = source.at[pl.ds(0, DEVICES - 1)]
        pltpu.make_async_copy(sent, sent, send_sem.at[phase]).wait()
    receive(results, returned, 1)


def finish_kernel(returned, ins, gq_hbm, gk_hbm, gv_hbm, gf_hbm, outs, sems):
    copies = []
    for half in range(2):
        rows = pl.ds(half * HALF, HALF)
        response = returned[:, half, :].T + ins[4, rows, :]
        back_signal = returned[:, 2 + half, :].T + ins[0, rows, :]
        outs[0, rows, :] = ins[3, rows, :] * response
        outs[1, rows, :] = back_signal * ins[2, rows, :]
        outs[2, rows, :] = back_signal * ins[1, rows, :]
        outs[3, rows, :] = returned[:, 4 + half, :].T
        for i, out in enumerate((gq_hbm, gk_hbm, gv_hbm, gf_hbm)):
            copies.append(pltpu.make_async_copy(outs.at[i, rows], out.at[rows], sems.at[i, half]))
            copies[-1].start()
    for copy in copies:
        copy.wait()


def local(queries, keys, values, cotangent, filt, skip):
    constants = tables()
    buffer = (DEVICES, ROWS, HALF)
    block = jax.ShapeDtypeStruct((BLOCK, DEVICES), jnp.float32)
    operands = (queries, keys, values, cotangent, filt, skip, *map(jnp.asarray, constants))
    returned, kept = pl.pallas_call(
        exchange_kernel,
        out_shape=(
            jax.ShapeDtypeStruct(buffer, jnp.float32),
            jax.ShapeDtypeStruct((5, BLOCK, DEVICES), jnp.float32),
        ),
        in_specs=[pl.BlockSpec(memory_space=pltpu.HBM)] * len(operands),
        out_specs=[pl.BlockSpec(memory_space=pltpu.VMEM)] * 2,
        scratch_shapes=[
            pltpu.VMEM((DEVICES,), jnp.float32),
            *[pltpu.VMEM(c.shape, jnp.float32) for c in constants],
            pltpu.VMEM((BLOCK, 3 * DEVICES), bfloat16),
            pltpu.VMEM((DEVICES, 3 * BLOCK), bfloat16),
            pltpu.VMEM((3 * BLOCK, BLOCK), bfloat16),
            pltpu.VMEM((3 * BLOCK, BLOCK), bfloat16),
            *[pltpu.VMEM(buffer, jnp.float32)] * 3,
            pltpu.SemaphoreType.DMA((6,)),
            pltpu.SemaphoreType.DMA((len(constants),)),
            pltpu.SemaphoreType.DMA((2,)),
            pltpu.SemaphoreType.DMA((2,)),
            pltpu.SemaphoreType.DMA((2,)),
        ],
        compiler_params=pltpu.CompilerParams(
            collective_id=0, has_side_effects=True, vmem_limit_bytes=40 * 1024 * 1024
        ),
        name="channel_convolutions",
    )(*[pltpu.with_memory_space_constraint(operand, pltpu.HBM) for operand in operands])
    return pl.pallas_call(
        finish_kernel,
        out_shape=(block,) * 4,
        in_specs=[pl.BlockSpec(memory_space=pltpu.VMEM)] * 2,
        out_specs=[pl.BlockSpec(memory_space=pltpu.HBM)] * 4,
        scratch_shapes=[pltpu.VMEM((4, BLOCK, DEVICES), jnp.float32), pltpu.SemaphoreType.DMA((4, 2))],
        compiler_params=pltpu.CompilerParams(vmem_limit_bytes=8 * 1024 * 1024),
        name="gates",
    )(returned, kept)


def solution(mesh):
    in_specs = (P(("sa", "sb"), None),) * 5 + (P(),)
    out_specs = (P(("sa", "sb"), None),) * 4
    return jax.shard_map(local, mesh=mesh, in_specs=in_specs, out_specs=out_specs, check_vma=False)
```

```python
import math

import jax
import jax.numpy as jnp
import numpy as np
from jax import lax
from jax.experimental import pallas as pl
from jax.experimental.pallas import tpu as pltpu
from jax.sharding import PartitionSpec as P

DEVICES = 128
BLOCK = 256
LENGTH = DEVICES * BLOCK
HALF = 128
ROWS = 6
LOGICAL = pl.DeviceIdType.LOGICAL
bfloat16 = jnp.bfloat16
RING = (0, 1, 2, 1)
BEHIND = (0.0, 2.0, 2.5, 2.9), (0.0, 0.8, 1.1, 1.0)

def tables():
    s = np.arange(DEVICES, dtype=np.float64)
    r = np.arange(BLOCK, dtype=np.float64)
    half = r[:HALF]
    outer = np.exp(-2j * np.pi * np.outer(s + 0.25, s) / DEVICES)
    turn = np.exp(-2j * np.pi * np.outer(s + 0.25, r) / LENGTH)
    inner = np.exp(-2j * np.pi * (np.outer(half, half) % HALF) / HALF)
    twist = np.exp(-2j * np.pi * half / BLOCK)
    scale = 1.0 / (LENGTH * math.sqrt(LENGTH))
    spread = np.concatenate([outer.real, outer.imag], 0)
    gather = np.concatenate([outer.real.T, outer.imag.T], 1) * scale
    inners = np.concatenate([inner.real, inner.imag], 1)
    turns = np.concatenate([turn.real, turn.imag], 0)
    twists = np.zeros((8, HALF))
    twists[0], twists[1] = twist.real, twist.imag
    return tuple(table.astype(np.float32) for table in (spread, gather, inners, turns, twists))


def hops(offset):
    return RING[(offset >> 1) & 3] + RING[(offset >> 3) & 3] + RING[(offset >> 5) & 3]


def returns():
    places = [(z, y, x, c) for z in range(4) for y in range(4) for x in range(4) for c in (1, 0)]
    return sorted(places, key=lambda p: (BEHIND[0][p[0]] + BEHIND[1][p[2]] - 0.64 * RING[p[1]], -p[3]))


ORDER = sorted(
    range(1, DEVICES),
    key=lambda s: (-(s >> 6), -RING[(s >> 3) & 3] - RING[(s >> 1) & 3] - 0.5 * ((s >> 5) & 1), (s * 77) % DEVICES),
)


def split(x):
    high = x.astype(bfloat16)
    low = (x - high.astype(jnp.float32)).astype(bfloat16)
    return high, low


def dot(a, b):
    return jnp.dot(a, b, preferred_element_type=jnp.float32)


def product(a, b, conjugate):
    ar, ai, br, bi = a[:, :HALF], a[:, HALF:], b[:, :HALF], b[:, HALF:]
    if conjugate:
        return jnp.concatenate([ar * br + ai * bi, ar * bi - ai * br], 1)
    return jnp.concatenate([ar * br - ai * bi, ar * bi + ai * br], 1)


def exchange_kernel(
    q_hbm, k_hbm, v_hbm, c_hbm, f_hbm, skip_hbm, spread_hbm, gather_hbm, inners_hbm, turns_hbm, twists_hbm,
    returned, ins,
    skip, spread_table, gather_table, inners, turns, twists, spread, gather, forward, inverse,
    outgoing, arrived, results,
    in_sem, const_sem, send_sem, recv_sem, own_sem,
):
    sa, sb = lax.axis_index("sa"), lax.axis_index("sb")
    me = sa * 16 + sb
    z, y = sa >> 1, ((sa & 1) << 1) | ((sb >> 1) & 1)
    x, core = sb >> 2, sb & 1
    sign = 1 - 2 * core
    z_steps = [(z ^ d) << 5 for d in range(4)]
    y_steps = [(((y + sign * d) & 2) << 3) | (((y + sign * d) & 1) << 1) for d in range(4)]
    x_steps = [((x + sign * d) & 3) << 2 for d in range(4)]
    cores = [core, 1 - core]

    def peer(offset):
        return z_steps[(offset >> 5) & 3] | y_steps[(offset >> 3) & 3] | x_steps[(offset >> 1) & 3] | cores[offset & 1]

    barrier = pltpu.get_barrier_semaphore()
    for offset in ORDER:
        pl.semaphore_signal(barrier, 1, device_id=peer(offset), device_id_type=LOGICAL)
    loads = [
        pltpu.make_async_copy(ref, ins.at[i], in_sem.at[i]) for i, ref in enumerate((q_hbm, k_hbm, v_hbm, c_hbm, f_hbm))
    ]
    loads.append(pltpu.make_async_copy(skip_hbm, skip, in_sem.at[5]))
    for load in loads:
        load.start()
    pairs = (
        (spread_hbm, spread_table), (gather_hbm, gather_table), (inners_hbm, inners), (turns_hbm, turns),
        (twists_hbm, twists),
    )
    constants = [pltpu.make_async_copy(a, b, const_sem.at[i]) for i, (a, b) in enumerate(pairs)]
    for load in constants:
        load.start()
    for load in loads:
        load.wait()
    gated, upstream = ins[1] * ins[2], ins[3] * ins[0]
    for number, signal in enumerate((gated, ins[4], upstream)):
        for half in range(2):
            outgoing[:, 2 * number + half, :] = signal[half * HALF : (half + 1) * HALF, :].T
    def send(source, target, phase, other):
        pltpu.make_async_remote_copy(
            src_ref=source.at[other],
            dst_ref=target.at[me],
            send_sem=send_sem.at[phase],
            recv_sem=recv_sem.at[phase],
            device_id=other,
            device_id_type=LOGICAL,
        ).start()

    def receive(source, target, phase):
        own = pltpu.make_async_copy(source.at[me], target.at[me], own_sem.at[phase])
        own.start()
        own.wait()
        landed = target.at[pl.ds(0, DEVICES - 1)]
        pltpu.make_async_copy(landed, landed, recv_sem.at[phase]).wait()

    pl.semaphore_wait(barrier, DEVICES - 1)
    for offset in ORDER:
        send(outgoing, arrived, 0, peer(offset))
    ins[0] = skip[...][None, :] * upstream
    ins[4] = skip[...][None, :] * gated

    for load in constants:
        load.wait()
    for table, target in ((spread_table, spread), (gather_table, gather)):
        high, low = split(table[...])
        width = table.shape[1]
        target[:, :width] = high
        target[:, width : 2 * width] = high
        target[:, 2 * width :] = low
    real_high, real_low = split(inners[:, :HALF])
    imag_high, imag_low = split(inners[:, HALF:])
    for base, real, imag in ((0, real_high, imag_high), (BLOCK, real_high, imag_high), (2 * BLOCK, real_low, imag_low)):
        for table, right, left in ((forward, imag, -imag), (inverse, -imag, imag)):
            table[base : base + HALF, :HALF] = real
            table[base : base + HALF, HALF:] = right
            table[base + HALF : base + BLOCK, :HALF] = left
            table[base + HALF : base + BLOCK, HALF:] = real

    receive(outgoing, arrived, 0)

    turn_real, turn_imag = turns[:HALF, :], turns[HALF:, :]
    twist_real, twist_imag = twists[0:1, :], twists[1:2, :]

    def along_blocks(matrix, x):
        high, low = split(x)
        return dot(matrix[...], jnp.concatenate([high, low, high], 0))

    def along_positions(x, matrix):
        high, low = split(x)
        return dot(jnp.concatenate([high, low, high], 1), matrix[...])

    def turned(first):
        real, imag = first[:HALF, :], first[HALF:, :]
        real, imag = real * turn_real - imag * turn_imag, real * turn_imag + imag * turn_real
        even = jnp.concatenate([real[:, :HALF] + real[:, HALF:], imag[:, :HALF] + imag[:, HALF:]], 1)
        real, imag = real[:, :HALF] - real[:, HALF:], imag[:, :HALF] - imag[:, HALF:]
        return even, jnp.concatenate([real * twist_real - imag * twist_imag, real * twist_imag + imag * twist_real], 1)

    def turned_back(even, odd):
        real, imag = odd[:, :HALF], odd[:, HALF:]
        real, imag = real * twist_real + imag * twist_imag, imag * twist_real - real * twist_imag
        real = jnp.concatenate([even[:, :HALF] + real, even[:, :HALF] - real], 1)
        imag = jnp.concatenate([even[:, HALF:] + imag, even[:, HALF:] - imag], 1)
        return jnp.concatenate([real * turn_real + imag * turn_imag, imag * turn_real - real * turn_imag], 0)

    firsts = [
        along_blocks(spread, jnp.concatenate([arrived[:, row, :], arrived[:, row + 1, :]], 1)) for row in (0, 2, 4)
    ]
    parts = [turned(first) for first in firsts]
    gated_part, filter_part, upstream_part = ([along_positions(half, forward) for half in part] for part in parts)
    products = [
        [product(a, b, conjugate) for a, b in zip(left, right)]
        for left, right, conjugate in (
            (filter_part, gated_part, False),
            (filter_part, upstream_part, True),
            (gated_part, upstream_part, True),
        )
    ]
    firsts = [[along_positions(half, inverse) for half in part] for part in products]
    parts = [turned_back(even, odd) for even, odd in firsts]
    for number, part in enumerate(parts):
        convolved = along_blocks(gather, part)
        for half in range(2):
            results[:, 2 * number + half, :] = convolved[:, half * HALF : (half + 1) * HALF]

    for to_z, step_y, to_x, step_core in returns():
        other = (to_z << 5) | y_steps[step_y] | (to_x << 2) | cores[step_core]
        if step_y == 0 and step_core == 0:
            pl.when(other != me)(lambda other=other: send(results, returned, 1, other))
        else:
            send(results, returned, 1, other)
    for phase, source in enumerate((outgoing, results)):
        sent = source.at[pl.ds(0, DEVICES - 1)]
        pltpu.make_async_copy(sent, sent, send_sem.at[phase]).wait()
    receive(results, returned, 1)


def finish_kernel(returned, ins, gq_hbm, gk_hbm, gv_hbm, gf_hbm, outs, sems):
    copies = []
    for half in range(2):
        rows = pl.ds(half * HALF, HALF)
        response = returned[:, half, :].T + ins[4, rows, :]
        back_signal = returned[:, 2 + half, :].T + ins[0, rows, :]
        outs[0, rows, :] = ins[3, rows, :] * response
        outs[1, rows, :] = back_signal * ins[2, rows, :]
        outs[2, rows, :] = back_signal * ins[1, rows, :]
        outs[3, rows, :] = returned[:, 4 + half, :].T
        for i, out in enumerate((gq_hbm, gk_hbm, gv_hbm, gf_hbm)):
            copies.append(pltpu.make_async_copy(outs.at[i, rows], out.at[rows], sems.at[i, half]))
            copies[-1].start()
    for copy in copies:
        copy.wait()


def local(queries, keys, values, cotangent, filt, skip):
    constants = tables()
    buffer = (DEVICES, ROWS, HALF)
    block = jax.ShapeDtypeStruct((BLOCK, DEVICES), jnp.float32)
    operands = (queries, keys, values, cotangent, filt, skip, *map(jnp.asarray, constants))
    returned, kept = pl.pallas_call(
        exchange_kernel,
        out_shape=(
            jax.ShapeDtypeStruct(buffer, jnp.float32),
            jax.ShapeDtypeStruct((5, BLOCK, DEVICES), jnp.float32),
        ),
        in_specs=[pl.BlockSpec(memory_space=pltpu.HBM)] * len(operands),
        out_specs=[pl.BlockSpec(memory_space=pltpu.VMEM)] * 2,
        scratch_shapes=[
            pltpu.VMEM((DEVICES,), jnp.float32),
            *[pltpu.VMEM(c.shape, jnp.float32) for c in constants],
            pltpu.VMEM((BLOCK, 3 * DEVICES), bfloat16),
            pltpu.VMEM((DEVICES, 3 * BLOCK), bfloat16),
            pltpu.VMEM((3 * BLOCK, BLOCK), bfloat16),
            pltpu.VMEM((3 * BLOCK, BLOCK), bfloat16),
            *[pltpu.VMEM(buffer, jnp.float32)] * 3,
            pltpu.SemaphoreType.DMA((6,)),
            pltpu.SemaphoreType.DMA((len(constants),)),
            pltpu.SemaphoreType.DMA((2,)),
            pltpu.SemaphoreType.DMA((2,)),
            pltpu.SemaphoreType.DMA((2,)),
        ],
        compiler_params=pltpu.CompilerParams(
            collective_id=0, has_side_effects=True, vmem_limit_bytes=40 * 1024 * 1024
        ),
        name="channel_convolutions",
    )(*[pltpu.with_memory_space_constraint(operand, pltpu.HBM) for operand in operands])
    return pl.pallas_call(
        finish_kernel,
        out_shape=(block,) * 4,
        in_specs=[pl.BlockSpec(memory_space=pltpu.VMEM)] * 2,
        out_specs=[pl.BlockSpec(memory_space=pltpu.HBM)] * 4,
        scratch_shapes=[pltpu.VMEM((4, BLOCK, DEVICES), jnp.float32), pltpu.SemaphoreType.DMA((4, 2))],
        compiler_params=pltpu.CompilerParams(vmem_limit_bytes=8 * 1024 * 1024),
        name="gates",
    )(returned, kept)


def solution(mesh):
    in_specs = (P(("sa", "sb"), None),) * 5 + (P(),)
    out_specs = (P(("sa", "sb"), None),) * 4
    return jax.shard_map(local, mesh=mesh, in_specs=in_specs, out_specs=out_specs, check_vma=False)
```

```python
import math

import jax
import jax.numpy as jnp
import numpy as np
from jax import lax
from jax.experimental import pallas as pl
from jax.experimental.pallas import tpu as pltpu
from jax.sharding import PartitionSpec as P

DEVICES = 128
BLOCK = 256
LENGTH = DEVICES * BLOCK
HALF = 128
ROWS = 6
LOGICAL = pl.DeviceIdType.LOGICAL
bfloat16 = jnp.bfloat16
RING = (0, 1, 2, 1)
BEHIND = (0.0, 2.0, 2.5, 2.9), (0.0, 0.8, 1.1, 1.0)

def tables():
    s = np.arange(DEVICES, dtype=np.float64)
    r = np.arange(BLOCK, dtype=np.float64)
    half = r[:HALF]
    outer = np.exp(-2j * np.pi * np.outer(s + 0.25, s) / DEVICES)
    turn = np.exp(-2j * np.pi * np.outer(s + 0.25, r) / LENGTH)
    inner = np.exp(-2j * np.pi * (np.outer(half, half) % HALF) / HALF)
    twist = np.exp(-2j * np.pi * half / BLOCK)
    scale = 1.0 / (LENGTH * math.sqrt(LENGTH))
    spread = np.concatenate([outer.real, outer.imag], 0)
    gather = np.concatenate([outer.real.T, outer.imag.T], 1) * scale
    inners = np.concatenate([inner.real, inner.imag], 1)
    turns = np.concatenate([turn.real, turn.imag], 0)
    twists = np.zeros((8, HALF))
    twists[0], twists[1] = twist.real, twist.imag
    return tuple(table.astype(np.float32) for table in (spread, gather, inners, turns, twists))


def hops(offset):
    return RING[(offset >> 1) & 3] + RING[(offset >> 3) & 3] + RING[(offset >> 5) & 3]


def returns():
    places = [(z, y, x, c) for z in range(4) for y in range(4) for x in range(4) for c in (1, 0)]
    return sorted(places, key=lambda p: (BEHIND[0][p[0]] + BEHIND[1][p[2]] - 0.64 * RING[p[1]], -p[3]))


ORDER = sorted(
    range(1, DEVICES),
    key=lambda s: (-(s >> 6), -RING[(s >> 3) & 3] - RING[(s >> 1) & 3] - 0.5 * ((s >> 5) & 1), (s * 77) % DEVICES),
)


def split(x):
    high = x.astype(bfloat16)
    low = (x - high.astype(jnp.float32)).astype(bfloat16)
    return high, low


def dot(a, b):
    return jnp.dot(a, b, preferred_element_type=jnp.float32)


def product(a, b, conjugate):
    ar, ai, br, bi = a[:, :HALF], a[:, HALF:], b[:, :HALF], b[:, HALF:]
    if conjugate:
        return jnp.concatenate([ar * br + ai * bi, ar * bi - ai * br], 1)
    return jnp.concatenate([ar * br - ai * bi, ar * bi + ai * br], 1)


def exchange_kernel(
    q_hbm, k_hbm, v_hbm, c_hbm, f_hbm, skip_hbm, spread_hbm, gather_hbm, inners_hbm, turns_hbm, twists_hbm,
    returned, ins,
    skip, spread_table, gather_table, inners, turns, twists, spread, gather, forward, inverse,
    outgoing, arrived, results,
    in_sem, const_sem, send_sem, recv_sem, own_sem,
):
    sa, sb = lax.axis_index("sa"), lax.axis_index("sb")
    me = sa * 16 + sb
    z, y = sa >> 1, ((sa & 1) << 1) | ((sb >> 1) & 1)
    x, core = sb >> 2, sb & 1
    sign = 1 - 2 * core
    z_steps = [(z ^ d) << 5 for d in range(4)]
    y_steps = [(((y + sign * d) & 2) << 3) | (((y + sign * d) & 1) << 1) for d in range(4)]
    x_steps = [((x + sign * d) & 3) << 2 for d in range(4)]
    cores = [core, 1 - core]

    def peer(offset):
        return z_steps[(offset >> 5) & 3] | y_steps[(offset >> 3) & 3] | x_steps[(offset >> 1) & 3] | cores[offset & 1]

    loads = [
        pltpu.make_async_copy(ref, ins.at[i], in_sem.at[i]) for i, ref in enumerate((q_hbm, k_hbm, v_hbm, c_hbm, f_hbm))
    ]
    loads.append(pltpu.make_async_copy(skip_hbm, skip, in_sem.at[5]))
    for load in loads:
        load.start()
    barrier = pltpu.get_barrier_semaphore()
    for offset in ORDER:
        pl.semaphore_signal(barrier, 1, device_id=peer(offset), device_id_type=LOGICAL)
    pairs = (
        (spread_hbm, spread_table), (gather_hbm, gather_table), (inners_hbm, inners), (turns_hbm, turns),
        (twists_hbm, twists),
    )
    constants = [pltpu.make_async_copy(a, b, const_sem.at[i]) for i, (a, b) in enumerate(pairs)]
    for load in constants:
        load.start()
    for load in loads:
        load.wait()
    gated, upstream = ins[1] * ins[2], ins[3] * ins[0]
    for number, signal in enumerate((gated, ins[4], upstream)):
        for half in range(2):
            outgoing[:, 2 * number + half, :] = signal[half * HALF : (half + 1) * HALF, :].T
    def send(source, target, phase, other):
        pltpu.make_async_remote_copy(
            src_ref=source.at[other],
            dst_ref=target.at[me],
            send_sem=send_sem.at[phase],
            recv_sem=recv_sem.at[phase],
            device_id=other,
            device_id_type=LOGICAL,
        ).start()

    def receive(source, target, phase):
        own = pltpu.make_async_copy(source.at[me], target.at[me], own_sem.at[phase])
        own.start()
        own.wait()
        landed = target.at[pl.ds(0, DEVICES - 1)]
        pltpu.make_async_copy(landed, landed, recv_sem.at[phase]).wait()

    pl.semaphore_wait(barrier, DEVICES - 1)
    for offset in ORDER:
        send(outgoing, arrived, 0, peer(offset))
    ins[0] = skip[...][None, :] * upstream
    ins[4] = skip[...][None, :] * gated

    for load in constants:
        load.wait()
    for table, target in ((spread_table, spread), (gather_table, gather)):
        high, low = split(table[...])
        width = table.shape[1]
        target[:, :width] = high
        target[:, width : 2 * width] = high
        target[:, 2 * width :] = low
    real_high, real_low = split(inners[:, :HALF])
    imag_high, imag_low = split(inners[:, HALF:])
    for base, real, imag in ((0, real_high, imag_high), (BLOCK, real_high, imag_high), (2 * BLOCK, real_low, imag_low)):
        for table, right, left in ((forward, imag, -imag), (inverse, -imag, imag)):
            table[base : base + HALF, :HALF] = real
            table[base : base + HALF, HALF:] = right
            table[base + HALF : base + BLOCK, :HALF] = left
            table[base + HALF : base + BLOCK, HALF:] = real

    receive(outgoing, arrived, 0)

    turn_real, turn_imag = turns[:HALF, :], turns[HALF:, :]
    twist_real, twist_imag = twists[0:1, :], twists[1:2, :]

    def along_blocks(matrix, x):
        high, low = split(x)
        return dot(matrix[...], jnp.concatenate([high, low, high], 0))

    def along_positions(x, matrix):
        high, low = split(x)
        return dot(jnp.concatenate([high, low, high], 1), matrix[...])

    def turned(first):
        real, imag = first[:HALF, :], first[HALF:, :]
        real, imag = real * turn_real - imag * turn_imag, real * turn_imag + imag * turn_real
        even = jnp.concatenate([real[:, :HALF] + real[:, HALF:], imag[:, :HALF] + imag[:, HALF:]], 1)
        real, imag = real[:, :HALF] - real[:, HALF:], imag[:, :HALF] - imag[:, HALF:]
        return even, jnp.concatenate([real * twist_real - imag * twist_imag, real * twist_imag + imag * twist_real], 1)

    def turned_back(even, odd):
        real, imag = odd[:, :HALF], odd[:, HALF:]
        real, imag = real * twist_real + imag * twist_imag, imag * twist_real - real * twist_imag
        real = jnp.concatenate([even[:, :HALF] + real, even[:, :HALF] - real], 1)
        imag = jnp.concatenate([even[:, HALF:] + imag, even[:, HALF:] - imag], 1)
        return jnp.concatenate([real * turn_real + imag * turn_imag, imag * turn_real - real * turn_imag], 0)

    firsts = [
        along_blocks(spread, jnp.concatenate([arrived[:, row, :], arrived[:, row + 1, :]], 1)) for row in (0, 2, 4)
    ]
    parts = [turned(first) for first in firsts]
    gated_part, filter_part, upstream_part = ([along_positions(half, forward) for half in part] for part in parts)
    products = [
        [product(a, b, conjugate) for a, b in zip(left, right)]
        for left, right, conjugate in (
            (filter_part, gated_part, False),
            (filter_part, upstream_part, True),
            (gated_part, upstream_part, True),
        )
    ]
    firsts = [[along_positions(half, inverse) for half in part] for part in products]
    parts = [turned_back(even, odd) for even, odd in firsts]
    for number, part in enumerate(parts):
        convolved = along_blocks(gather, part)
        for half in range(2):
            results[:, 2 * number + half, :] = convolved[:, half * HALF : (half + 1) * HALF]

    own = pltpu.make_async_copy(results.at[me], returned.at[me], own_sem.at[1])
    own.start()
    for to_z, step_y, to_x, step_core in returns():
        other = (to_z << 5) | y_steps[step_y] | (to_x << 2) | cores[step_core]
        if step_y == 0 and step_core == 0:
            pl.when(other != me)(lambda other=other: send(results, returned, 1, other))
        else:
            send(results, returned, 1, other)
    for phase, source in enumerate((outgoing, results)):
        sent = source.at[pl.ds(0, DEVICES - 1)]
        pltpu.make_async_copy(sent, sent, send_sem.at[phase]).wait()
    own.wait()
    landed = returned.at[pl.ds(0, DEVICES - 1)]
    pltpu.make_async_copy(landed, landed, recv_sem.at[1]).wait()


def finish_kernel(returned, ins, gq_hbm, gk_hbm, gv_hbm, gf_hbm, outs, sems):
    copies = []
    for half in range(2):
        rows = pl.ds(half * HALF, HALF)
        response = returned[:, half, :].T + ins[4, rows, :]
        back_signal = returned[:, 2 + half, :].T + ins[0, rows, :]
        outs[0, rows, :] = ins[3, rows, :] * response
        outs[1, rows, :] = back_signal * ins[2, rows, :]
        outs[2, rows, :] = back_signal * ins[1, rows, :]
        outs[3, rows, :] = returned[:, 4 + half, :].T
        for i, out in enumerate((gq_hbm, gk_hbm, gv_hbm, gf_hbm)):
            copies.append(pltpu.make_async_copy(outs.at[i, rows], out.at[rows], sems.at[i, half]))
            copies[-1].start()
    for copy in copies:
        copy.wait()


def local(queries, keys, values, cotangent, filt, skip):
    constants = tables()
    buffer = (DEVICES, ROWS, HALF)
    block = jax.ShapeDtypeStruct((BLOCK, DEVICES), jnp.float32)
    operands = (queries, keys, values, cotangent, filt, skip, *map(jnp.asarray, constants))
    returned, kept = pl.pallas_call(
        exchange_kernel,
        out_shape=(
            jax.ShapeDtypeStruct(buffer, jnp.float32),
            jax.ShapeDtypeStruct((5, BLOCK, DEVICES), jnp.float32),
        ),
        in_specs=[pl.BlockSpec(memory_space=pltpu.HBM)] * len(operands),
        out_specs=[pl.BlockSpec(memory_space=pltpu.VMEM)] * 2,
        scratch_shapes=[
            pltpu.VMEM((DEVICES,), jnp.float32),
            *[pltpu.VMEM(c.shape, jnp.float32) for c in constants],
            pltpu.VMEM((BLOCK, 3 * DEVICES), bfloat16),
            pltpu.VMEM((DEVICES, 3 * BLOCK), bfloat16),
            pltpu.VMEM((3 * BLOCK, BLOCK), bfloat16),
            pltpu.VMEM((3 * BLOCK, BLOCK), bfloat16),
            *[pltpu.VMEM(buffer, jnp.float32)] * 3,
            pltpu.SemaphoreType.DMA((6,)),
            pltpu.SemaphoreType.DMA((len(constants),)),
            pltpu.SemaphoreType.DMA((2,)),
            pltpu.SemaphoreType.DMA((2,)),
            pltpu.SemaphoreType.DMA((2,)),
        ],
        compiler_params=pltpu.CompilerParams(
            collective_id=0, has_side_effects=True, vmem_limit_bytes=40 * 1024 * 1024
        ),
        name="channel_convolutions",
    )(*[pltpu.with_memory_space_constraint(operand, pltpu.HBM) for operand in operands])
    return pl.pallas_call(
        finish_kernel,
        out_shape=(block,) * 4,
        in_specs=[pl.BlockSpec(memory_space=pltpu.VMEM)] * 2,
        out_specs=[pl.BlockSpec(memory_space=pltpu.HBM)] * 4,
        scratch_shapes=[pltpu.VMEM((4, BLOCK, DEVICES), jnp.float32), pltpu.SemaphoreType.DMA((4, 2))],
        compiler_params=pltpu.CompilerParams(vmem_limit_bytes=8 * 1024 * 1024),
        name="gates",
    )(returned, kept)


def solution(mesh):
    in_specs = (P(("sa", "sb"), None),) * 5 + (P(),)
    out_specs = (P(("sa", "sb"), None),) * 4
    return jax.shard_map(local, mesh=mesh, in_specs=in_specs, out_specs=out_specs, check_vma=False)
```
